256 devices in a mesh: grp: 8 (over y_lo, x), tp: 32 (over y_hi, z, core).
Axes of the slice: x: 4, y: 4 (y_hi: 2, y_lo: 2; y = y_hi * 2 + y_lo), z: 8, core: 2. Of those that a mesh axis runs over, the one named last changes fastest.
Arguments:
- prompt_q: bfloat16 [16384, 4096], P(('grp', 'tp')), may hold values from -8 to 8
- prompt_k: bfloat16 [16384, 1024], P(('grp', 'tp')), may hold values from -150 to 150
- prompt_v: bfloat16 [16384, 1024], P(('grp', 'tp')), may hold values from -6 to 6
- lengths: int32 [8], P('grp'), may hold values from 8192 to 16384, as said below
- sample_states: bfloat16 [128, 2, 5120], P('grp'), may hold values from -6 to 6
- norm_gain: bfloat16 [5120], replicated, may hold values from 0.099609375 to 1.8984375
- w_query: bfloat16 [5120, 4096], P(None, 'tp'), may hold values from -0.15625 to 0.15625
- b_query: bfloat16 [4096], P('tp'), may hold values from -3 to 3
- w_key: bfloat16 [5120, 1024], P(None, 'tp'), may hold values from -0.625 to 0.625
- b_key: bfloat16 [1024], P('tp'), may hold values from -3 to 3
- w_value: bfloat16 [5120, 1024], P(None, 'tp'), may hold values from -0.078125 to 0.078125
- b_value: bfloat16 [1024], P('tp'), may hold values from -3 to 3
- w_out: bfloat16 [4096, 5120], P('tp'), may hold values from -0.09375 to 0.09375
Outputs:
- prefill_mixed: bfloat16 [16384, 4096], P(('grp', 'tp'))
- decode_out: bfloat16 [128, 2, 5120], P('grp')
The draws below stay inside these ranges and needn't reach their ends.
Inputs may be any that keep to these rules, and one draw needn't show every extreme that they name: `lengths`: one group's length is 16384 in every draw.
All inputs are finite; a program needn't handle non-finite values.
Results may differ from the reference program's by a relative error of at most 0.014.
The reference program's roundings to bfloat16 on the way count: a program that leaves them out, or rounds other values in their place, can miss the bound.
Values may be sent and summed in bfloat16 or wider, within the bound.
A program may use at most 128 MiB of HBM per device.

```python
import math
import jax
import jax.numpy as jnp
from jax import lax

D = 5120
HEADS = 32
KV_HEADS = 8
HEAD_DIM = 128
SAMPLES = 16
STEPS = 2
PROMPT = 16384
ROWS = 128
N_GRP = 8


def draw_prompt_k(key, part):
    key = jax.random.fold_in(key, 17)
    noise_key = jax.random.fold_in(key, 0)
    columns = KV_HEADS * HEAD_DIM
    return (1.5 * jax.random.truncated_normal(noise_key, -4.0, 4.0, (PROMPT, columns), jnp.float32)).astype(jnp.bfloat16)


def draw_lengths(key, part):
    key = jax.random.fold_in(key, 29)
    value_key, pick_key = jax.random.split(key)
    drawn = jax.random.randint(value_key, (N_GRP,), PROMPT // 2, PROMPT + 1)
    chosen = jax.random.randint(pick_key, (), 0, N_GRP)
    return jnp.where(jnp.arange(N_GRP) == chosen, PROMPT, drawn).astype(jnp.int32)


def block_scale(stream_key, extent, cuts, smallest, high):
    loudness = 1.0
    for dim, blocks in cuts:
        draws = jax.random.uniform(jax.random.fold_in(jax.random.fold_in(stream_key, 6), dim), (blocks,), jnp.float32, smallest / len(cuts), high / len(cuts))
        loudness = loudness * jnp.repeat(jnp.exp(draws), extent[dim] // blocks).reshape((-1,) + (1,) * (len(extent) - 1 - dim))
    return loudness


def bell_draw(stream_key, extent, width, limit, pieces=(), kind=jnp.bfloat16):
    gain = block_scale(stream_key, extent, pieces, -0.22, 0.18) if pieces else 1.0
    values = jax.random.normal(stream_key, extent, jnp.float32) * width * gain
    return jnp.minimum(jnp.maximum(values, -limit), limit).astype(kind)


def setup_inputs(seed: int = 0) -> dict:
    streams_of = jax.random.split(jax.random.key(seed), 14)
    return {
        "prompt_q": bell_draw(streams_of[0], (PROMPT, HEADS * HEAD_DIM), 2.0, 8.0, ((0, 256),)),
        "prompt_k": draw_prompt_k(jax.random.fold_in(streams_of[13], 71), 0),
        "prompt_v": bell_draw(streams_of[2], (PROMPT, KV_HEADS * HEAD_DIM), 1.0, 6.0, ((0, 256),)),
        "lengths": draw_lengths(jax.random.fold_in(streams_of[13], 71), 0),
        "sample_states": bell_draw(streams_of[4], (ROWS, STEPS, D), 1.0, 6.0, ((0, 8),)),
        "norm_gain": jnp.clip(1.0 + 0.18 * jax.random.normal(streams_of[5], (D,), jnp.float32), 0.099609375, 1.8984375).astype(jnp.bfloat16),
        "w_query": bell_draw(streams_of[6], (D, HEADS * HEAD_DIM), (D // 4) ** -0.5, 0.15625, ((1, 32),)),
        "b_query": bell_draw(streams_of[7], (HEADS * HEAD_DIM,), 0.5, 3.0, ((0, 32),)),
        "w_key": bell_draw(streams_of[8], (D, KV_HEADS * HEAD_DIM), (D // 64) ** -0.5, 0.625, ((1, 32),)),
        "b_key": bell_draw(streams_of[9], (KV_HEADS * HEAD_DIM,), 0.5, 3.0, ((0, 32),)),
        "w_value": bell_draw(streams_of[10], (D, KV_HEADS * HEAD_DIM), D ** -0.5, 0.078125, ((1, 32),)),
        "b_value": bell_draw(streams_of[11], (KV_HEADS * HEAD_DIM,), 0.5, 3.0, ((0, 32),)),
        "w_out": bell_draw(streams_of[12], (HEADS * HEAD_DIM, D), (HEADS * HEAD_DIM) ** -0.5, 0.09375, ((0, 32),)),
    }


epsilon = 1e-06
rope_base = 1000000.0

def rotate(tensor, position):
    half_dim = HEAD_DIM // 2
    frequency = rope_base ** (-(2.0 * jnp.arange(half_dim, dtype=jnp.float32)) / HEAD_DIM)
    angles = position[..., None] * frequency
    cosine_table = jnp.cos(angles)
    sine_table = jnp.sin(angles)
    front_part = tensor[..., :half_dim]
    back_part = tensor[..., half_dim:]
    return jnp.concatenate([front_part * cosine_table - back_part * sine_table, back_part * cosine_table + front_part * sine_table], axis=-1)

def prompt_attention(prompt_q, prompt_k, prompt_v):
    group_size = HEADS // KV_HEADS
    scaling = HEAD_DIM ** (-0.5)
    head_queries = jnp.transpose(prompt_q.reshape(PROMPT, HEADS, HEAD_DIM), (1, 0, 2))
    head_keys = jnp.repeat(jnp.transpose(prompt_k.reshape(PROMPT, KV_HEADS, HEAD_DIM), (1, 0, 2)), group_size, axis=0)
    head_values = jnp.repeat(jnp.transpose(prompt_v.reshape(PROMPT, KV_HEADS, HEAD_DIM), (1, 0, 2)), group_size, axis=0)
    block_width = math.gcd(PROMPT, 512)
    outputs = []
    for block_no in range(PROMPT // block_width):
        start_row = block_no * block_width
        stop_row = start_row + block_width
        query_pos = start_row + jnp.arange(block_width, dtype=jnp.int32)
        key_pos = jnp.arange(stop_row, dtype=jnp.int32)
        allowed = key_pos[None, :] <= query_pos[:, None]

        def one_head(operands, allowed=allowed):
            queries, key_rows, value_rows = operands
            scores = jnp.dot(queries, key_rows.T, preferred_element_type=jnp.float32) * scaling
            highest = lax.optimization_barrier(jnp.max(jnp.where(allowed, scores, -jnp.inf), axis=-1))
            weights = jnp.where(allowed, jnp.exp(scores - highest[:, None]), 0.0)
            weight_sum = lax.optimization_barrier(jnp.sum(weights, axis=-1))
            mixed_rows = jnp.dot(weights.astype(jnp.bfloat16), value_rows, preferred_element_type=jnp.float32)
            return mixed_rows / weight_sum[:, None]
        outputs.append(lax.map(one_head, (head_queries[:, start_row:stop_row], head_keys[:, :stop_row], head_values[:, :stop_row])))
    mixed_all = jnp.concatenate(outputs, axis=1)
    return jnp.transpose(mixed_all, (1, 0, 2)).reshape(PROMPT, HEADS * HEAD_DIM).astype(jnp.bfloat16)

def decode_block(lengths, sample_states, norm_gain, w_query, b_query, w_key, b_key, w_value, b_value, w_out, prompt_k, prompt_v):
    group_size = HEADS // KV_HEADS
    scaling = HEAD_DIM ** (-0.5)
    states = sample_states.astype(jnp.float32)
    normed = (states * lax.rsqrt(lax.optimization_barrier(jnp.mean(states * states, axis=-1, keepdims=True)) + epsilon) * norm_gain.astype(jnp.float32)).astype(jnp.bfloat16)
    flat_rows = normed.reshape(ROWS * STEPS, D)
    query = jnp.dot(flat_rows, w_query, preferred_element_type=jnp.float32) + b_query.astype(jnp.float32)
    new_key = jnp.dot(flat_rows, w_key, preferred_element_type=jnp.float32) + b_key.astype(jnp.float32)
    step_value = (jnp.dot(flat_rows, w_value, preferred_element_type=jnp.float32) + b_value.astype(jnp.float32)).astype(jnp.bfloat16)
    group_length = jnp.repeat(lengths, SAMPLES)
    positions = (group_length[:, None] + jnp.arange(STEPS, dtype=jnp.int32)[None, :]).astype(jnp.float32)[:, :, None]
    step_query = rotate(query.reshape(ROWS, STEPS, HEADS, HEAD_DIM), positions).astype(jnp.bfloat16)
    step_key = jnp.repeat(rotate(new_key.reshape(ROWS, STEPS, KV_HEADS, HEAD_DIM), positions).astype(jnp.bfloat16), group_size, axis=2)
    step_vals = jnp.repeat(step_value.reshape(ROWS, STEPS, KV_HEADS, HEAD_DIM), group_size, axis=2)
    head_keys = jnp.repeat(prompt_k.reshape(PROMPT, KV_HEADS, HEAD_DIM), group_size, axis=1).astype(jnp.float32)
    head_values = jnp.repeat(prompt_v.reshape(PROMPT, KV_HEADS, HEAD_DIM), group_size, axis=1).astype(jnp.float32)
    own_allowed = (jnp.arange(STEPS)[None, :] <= jnp.arange(STEPS)[:, None])[None, None]

    def one_group(operands):
        queries, own_keys, own_values, length_limit = operands
        query_float = queries.astype(jnp.float32)
        prompt_scores = jnp.einsum('sahd,khd->hsak', query_float, head_keys, precision=lax.Precision.HIGHEST) * scaling
        prompt_allowed = (jnp.arange(PROMPT, dtype=jnp.int32) < length_limit)[None, None, None, :]
        own_scores = jnp.einsum('sahd,sbhd->hsab', query_float, own_keys.astype(jnp.float32), precision=lax.Precision.HIGHEST) * scaling
        highest = jnp.maximum(lax.optimization_barrier(jnp.max(jnp.where(prompt_allowed, prompt_scores, -jnp.inf), axis=-1)), lax.optimization_barrier(jnp.max(jnp.where(own_allowed, own_scores, -jnp.inf), axis=-1)))
        prompt_weights = jnp.where(prompt_allowed, jnp.exp(prompt_scores - highest[..., None]), 0.0)
        own_weights = jnp.where(own_allowed, jnp.exp(own_scores - highest[..., None]), 0.0)
        weight_sum = lax.optimization_barrier(jnp.sum(prompt_weights, axis=-1)) + lax.optimization_barrier(jnp.sum(own_weights, axis=-1))
        prompt_rounded = lax.optimization_barrier(prompt_weights.astype(jnp.bfloat16)).astype(jnp.float32)
        own_rounded = lax.optimization_barrier(own_weights.astype(jnp.bfloat16)).astype(jnp.float32)
        mixed_rows = jnp.einsum('hsak,khd->sahd', prompt_rounded, head_values, precision=lax.Precision.HIGHEST)
        mixed_rows = mixed_rows + jnp.einsum('hsab,sbhd->sahd', own_rounded, own_values.astype(jnp.float32), precision=lax.Precision.HIGHEST)
        mixed_rows = mixed_rows / jnp.transpose(weight_sum, (1, 2, 0))[..., None]
        attended = mixed_rows.astype(jnp.bfloat16).reshape(SAMPLES * STEPS, HEADS * HEAD_DIM)
        return jnp.dot(attended, w_out, preferred_element_type=jnp.float32).astype(jnp.bfloat16).reshape(SAMPLES, STEPS, D)
    result = lax.map(one_group, (step_query.reshape(N_GRP, SAMPLES, STEPS, HEADS, HEAD_DIM), step_key.reshape(N_GRP, SAMPLES, STEPS, HEADS, HEAD_DIM), step_vals.reshape(N_GRP, SAMPLES, STEPS, HEADS, HEAD_DIM), lengths))
    return result.reshape(ROWS, STEPS, D)

def reference(prompt_q, prompt_k, prompt_v, lengths, sample_states, norm_gain, w_query, b_query, w_key, b_key, w_value, b_value, w_out):
    prefill_mixed = prompt_attention(prompt_q, prompt_k, prompt_v)
    decode_out = decode_block(lengths, sample_states, norm_gain, w_query, b_query, w_key, b_key, w_value, b_value, w_out, prompt_k, prompt_v)
    return (prefill_mixed, decode_out)
```

```python
import math

import jax
import jax.numpy as jnp
from jax import lax
from jax.experimental import pallas as pl
from jax.experimental.pallas import tpu as pltpu
from jax.sharding import PartitionSpec as P

HEADS = 32
KV_HEADS = 8
HEAD_DIM = 128
STEPS = 2
EPSILON = 1e-06
ROPE_BASE = 1000000.0
MESH = pl.DeviceIdType.MESH
F32 = jnp.float32
BF16 = jnp.bfloat16
NEG = -1e30
C = math.log2(math.e) / math.sqrt(HEAD_DIM)
NT = (((1,), (1,)), ((), ()))
CHUNK = 1024
TILE = 256


def dot_nt(a, b):
    return lax.dot_general(a, b, NT, preferred_element_type=F32)


def kernel(
    q_ref, k_ref, v_ref, st_ref, gain_ref, cos_ref, sin_ref, len_ref,
    wq_ref, bq_ref, wk_ref, bk_ref, wv_ref, bv_ref, wo_ref,
    out_ref, dec_ref,
    kvbuf, qbuf, obuf, S, acc, mx, ls,
    wq_v, wk_v, wv_v, wo_v, dq_own, dq, kvp_own, kvp, pmsg, part, opart, rs0, hsum, rs, fbuf, fsib,
    dacc, dmx, dls,
    w_sem, kv0_recv, kv0_loc, kv0_send, q_recv, q_send, ag_recv, ag_send, sib_recv, sib_send,
    o_recv, o_send, dq_recv, dq_send, kvp_recv, kvp_send, part_recv, part_send,
    rs0_recv, rs0_send, rs_recv, rs_send, f_recv, f_send, fs_recv, fs_send,
):
    g = lax.axis_index("grp")
    t = lax.axis_index("tp")
    x, ylo = lax.rem(g, 4), lax.div(g, 4)
    yhi, z, core = lax.div(t, 16), lax.rem(lax.div(t, 2), 8), lax.rem(t, 2)
    y = yhi * 2 + ylo
    own = (ylo * 4 + x) * 2 + yhi

    def dev(xx, yy, zz, cc):
        return {"grp": lax.rem(yy, 2) * 4 + xx, "tp": lax.div(yy, 2) * 16 + zz * 2 + cc}

    def flip(bit, by):
        return bit + by * (1 - 2 * bit)

    def column(by):
        return x + by * (3 - 2 * x), y + by * (3 - 2 * y)

    def rcopy(src, dst, send, recv, to):
        return pltpu.make_async_remote_copy(
            src_ref=src, dst_ref=dst, send_sem=send, recv_sem=recv, device_id=to, device_id_type=MESH
        )

    def drain(ref, sem):
        pltpu.make_async_copy(ref, ref, sem).wait()

    def head_cols(ref, h, width=HEAD_DIM):
        return ref.at[:, pl.ds(pl.multiple_of(h * width, width), width)]

    weights = [
        pltpu.make_async_copy(a, b, w_sem.at[i])
        for i, (a, b) in enumerate(((wq_ref, wq_v), (wk_ref, wk_v), (wv_ref, wv_v), (wo_ref, wo_v)))
    ]
    for w in weights:
        w.start()

    barrier = pltpu.get_barrier_semaphore()

    def greet(to):
        pl.semaphore_signal(barrier, inc=1, device_id=to, device_id_type=MESH)

    y2 = lax.rem(y + 2, 4)
    for dc in range(2):
        for dz in range(8):
            zz, cc = lax.rem(z + dz, 8), flip(core, dc)
            if dz or dc:
                greet(dev(x, y, zz, cc))
            greet(dev(3 - x, 3 - y, zz, cc))
            greet(dev(x, y2, zz, cc))
    for d in (1, 3):
        greet(dev(lax.rem(x + d, 4), y, z, core))
        greet(dev(x, lax.rem(y + d, 4), z, core))
    pl.semaphore_wait(barrier, 51)

    for dz in range(1, 8):
        zz = lax.rem(z + dz, 8)
        for kv, ref in enumerate((k_ref, v_ref)):
            rcopy(
                head_cols(ref, zz), kvbuf.at[kv, own, z, core], kv0_send.at[kv], kv0_recv.at[kv],
                dev(x, y, zz, core),
            ).start()
    kv_local = [
        pltpu.make_async_copy(head_cols(ref, z), kvbuf.at[kv, own, z, core], kv0_loc.at[kv])
        for kv, ref in enumerate((k_ref, v_ref))
    ]
    for c in kv_local:
        c.start()
    for dz in range(8):
        zz = lax.rem(z + dz, 8)
        for dp in range(2):
            px, py = column(dp)
            for dc in range(2):
                cc = flip(core, dc)
                src = head_cols(q_ref, 4 * zz + 2 * flip(ylo, dp) + cc)
                dst = qbuf.at[ylo, z, core]
                if dz or dp or dc:
                    rcopy(src, dst, q_send.at[dp], q_recv.at[ylo], dev(px, py, zz, cc)).start()
                else:
                    pltpu.make_async_copy(src, dst, q_recv.at[ylo]).start()

    states = st_ref[...].astype(F32)
    scale = lax.rsqrt(jnp.mean(states * states, axis=1, keepdims=True) + EPSILON)
    normed = (states * scale * gain_ref[...].astype(F32)).astype(BF16)
    for w in weights:
        w.wait()
    cosine, sine = cos_ref[...], sin_ref[...]

    def rotate(value):
        return value * cosine + pltpu.roll(value, HEAD_DIM // 2, 1) * sine

    query = jnp.dot(normed, wq_v[...], preferred_element_type=F32) + bq_ref[...].astype(F32)
    dq_own[...] = rotate(query).astype(BF16)
    quarter = lax.rem(t, 4)
    spread = (
        lax.broadcasted_iota(jnp.int32, (32, HEAD_DIM), 1)
        == lax.broadcasted_iota(jnp.int32, (32, HEAD_DIM), 0) + quarter * 32
    ).astype(F32)
    for i, (w, b) in enumerate(((wk_v, bk_ref), (wv_v, bv_ref))):
        narrow = jnp.dot(normed, w[...], preferred_element_type=F32) + b[...].astype(F32)
        kvp_own[i] = jnp.dot(narrow, spread, precision=lax.Precision.HIGHEST, preferred_element_type=F32)

    late = []

    def to_tp(target, src, dst, send, recv):
        @pl.when(target != t)
        def _():
            rcopy(src, dst, send, recv, {"grp": g, "tp": target}).start()

        @pl.when(target == t)
        def _():
            pltpu.make_async_copy(src, dst, recv).start()

        late.append((target, src, send))

    for i in range(4):
        target = (i // 2) * 16 + lax.div(t, 4) * 2 + i % 2
        to_tp(target, dq_own, dq.at[quarter], dq_send.at[i], dq_recv.at[quarter])
    for m in range(1, 4):
        target = lax.div(t, 4) * 4 + lax.rem(quarter + m, 4)
        rcopy(kvp_own, kvp.at[m - 1], kvp_send.at[m - 1], kvp_recv.at[m - 1], {"grp": g, "tp": target}).start()

    def place(o1, o2):
        ox, oy = (1 - core) * o1 + core * o2, core * o1 + (1 - core) * o2
        return lax.rem(x + ox, 4), lax.rem(y + oy, 4)

    def chunk_of(o1, o2):
        xx, yy = place(o1, o2)
        return (lax.rem(yy, 2) * 4 + xx) * 2 + lax.div(yy, 2)

    def block(o1, o2, kv=None):
        return kvbuf.at[slice(None) if kv is None else kv, chunk_of(o1, o2), :, core]

    def toward(axis, step):
        xx, yy = place(step, 0) if axis == 1 else place(0, step)
        return dev(xx, yy, z, core)

    sends = []

    def send(src, sem, recv, to):
        c = rcopy(src, src, sem, recv, to)
        c.start()
        sends.append(c)

    sibling = dev(x, y, z, 1 - core)

    def to_sibling(o1, o2):
        send(block(o1, o2), sib_send.at[o1, o2], sib_recv.at[o1, o2], sibling)

    def from_sibling(o1, o2):
        drain(kvbuf.at[:, chunk_of(o1, o2), :, 1 - core], sib_recv.at[o2, o1])

    def open_axis1():
        send(block(0, 0), ag_send.at[0, 0], ag_recv.at[3, 0, 0], toward(1, 1))
        send(block(0, 0), ag_send.at[0, 1], ag_recv.at[1, 0, 0], toward(1, 3))

    def open_axis2(o1):
        send(block(o1, 0), ag_send.at[1 + o1, 0], ag_recv.at[o1, 3, 0], toward(2, 1))
        send(block(o1, 0), ag_send.at[1 + o1, 1], ag_recv.at[o1, 1, 0], toward(2, 3))

    def pass_axis1():
        drain(block(3, 0), ag_recv.at[3, 0, 0])
        send(block(3, 0, 0), ag_send.at[0, 2], ag_recv.at[2, 0, 0], toward(1, 1))
        drain(block(1, 0), ag_recv.at[1, 0, 0])
        send(block(1, 0, 1), ag_send.at[0, 3], ag_recv.at[2, 0, 1], toward(1, 3))

    def pass_axis2(o1):
        drain(block(o1, 3), ag_recv.at[o1, 3, 0])
        send(block(o1, 3, 0), ag_send.at[1 + o1, 2], ag_recv.at[o1, 2, 0], toward(2, 1))
        drain(block(o1, 1), ag_recv.at[o1, 1, 0])
        send(block(o1, 1, 1), ag_send.at[1 + o1, 3], ag_recv.at[o1, 2, 1], toward(2, 3))
        to_sibling(o1, 3)
        to_sibling(o1, 1)

    def end_axis(o1, o2):
        for kv in range(2):
            drain(block(o1, o2, kv), ag_recv.at[o1, o2, kv])
        to_sibling(o1, o2)

    for kv in range(2):
        kv_local[kv].wait()
        drain(kvbuf.at[kv, own, pl.ds(0, 7), core], kv0_recv.at[kv])
    open_axis1()
    open_axis2(0)
    to_sibling(0, 0)
    pass_axis1()
    open_axis2(1)
    open_axis2(3)
    to_sibling(1, 0)
    to_sibling(3, 0)
    pass_axis2(0)
    end_axis(2, 0)
    open_axis2(2)
    pass_axis2(1)
    pass_axis2(3)
    end_axis(0, 2)
    pass_axis2(2)
    end_axis(1, 2)
    end_axis(3, 2)
    end_axis(2, 2)
    for o1 in range(4):
        for o2 in range(4):
            from_sibling(o1, o2)

    for slot in range(2):
        drain(qbuf.at[slot], q_recv.at[slot])
    acc[...] = jnp.zeros_like(acc)
    mx[...] = jnp.full_like(mx, NEG)
    ls[...] = jnp.zeros_like(ls)
    low = own + ylo * (15 - 2 * own)

    def unit(slot, cc, diagonal):
        tiles = CHUNK // TILE
        keys = kvbuf[0, cc].reshape(CHUNK, HEAD_DIM)
        values = kvbuf[1, cc].reshape(CHUNK, HEAD_DIM)
        held = {}

        def scores(i):
            width = (i + 1) * TILE if diagonal else CHUNK
            rows = pl.ds(i * TILE, TILE)
            s = dot_nt(qbuf[slot, 2 * i : 2 * i + 2].reshape(TILE, HEAD_DIM), keys[:width])
            if diagonal:
                r = lax.broadcasted_iota(jnp.int32, (TILE, width), 0) + i * TILE
                s = jnp.where(lax.broadcasted_iota(jnp.int32, (TILE, width), 1) <= r, s, NEG)
            S[i % 2, :, :width] = s
            old = mx[slot, rows, :]
            new = jnp.maximum(old, jnp.max(s, axis=1, keepdims=True))
            mx[slot, rows, :] = new
            held[i] = (old, new)

        def mix(i):
            width = (i + 1) * TILE if diagonal else CHUNK
            rows = pl.ds(i * TILE, TILE)
            old, new = held.pop(i)
            p = jnp.exp2(S[i % 2, :, :width] * C - (new * C)[:, :1])
            shrink = jnp.exp2((old - new) * C)
            ls[slot, rows, :] = ls[slot, rows, :] * shrink + jnp.sum(p, axis=1, keepdims=True)
            gained = jnp.dot(p.astype(BF16), values[:width], preferred_element_type=F32)
            acc[slot, rows, :] = acc[slot, rows, :] * shrink + gained

        scores(0)
        for i in range(tiles):
            if i + 1 < tiles:
                scores(i + 1)
            mix(i)

    def visit(i, carry):
        cc, slot = lax.div(i, 2), lax.rem(i, 2)
        last = low + slot * (15 - 2 * low)

        @pl.when(cc < last)
        def _():
            unit(slot, cc, False)

        @pl.when(cc == last)
        def _():
            unit(slot, cc, True)

        return carry

    lax.fori_loop(0, 32, visit, 0)

    for slot in range(2):
        obuf[slot] = (acc[slot] / ls[slot]).astype(BF16).reshape(8, 2, 64, HEAD_DIM)
        dp = flip(slot, ylo)
        px, py = column(dp)
        for dz in range(8):
            zz = lax.rem(z + dz, 8)
            for dc in range(2):
                cc = flip(core, dc)
                src = obuf.at[slot, zz, cc]
                dst = head_cols(out_ref, 4 * z + 2 * ylo + core)

                def away(src=src, dst=dst, to=dev(px, py, zz, cc), dp=dp):
                    rcopy(src, dst, o_send.at[dp], o_recv, to).start()

                if dz or dc:
                    away()
                else:
                    pl.when(dp == 1)(away)

                    @pl.when(dp == 0)
                    def _():
                        pltpu.make_async_copy(src, dst, o_recv).start()

    for i in range(4):
        drain(dq.at[i], dq_recv.at[i])
    dacc[...] = jnp.zeros_like(dacc)
    dmx[...] = jnp.full_like(dmx, NEG)
    dls[...] = jnp.zeros_like(dls)
    limit = len_ref[0]
    yq = lax.rem(y + core, 4)

    def decode_visit(i, carry):
        cc = (lax.rem(yq, 2) * 4 + i) * 2 + lax.div(yq, 2)
        s = dot_nt(dq[...].reshape(128, HEAD_DIM), kvbuf[0, cc].reshape(CHUNK, HEAD_DIM))
        allowed = lax.broadcasted_iota(jnp.int32, (128, CHUNK), 1) + cc * CHUNK < limit
        s = jnp.where(allowed, s, NEG)
        old = dmx[...]
        new = jnp.maximum(old, jnp.max(s, axis=1, keepdims=True))
        dmx[...] = new
        p = jnp.where(allowed, jnp.exp2(s * C - (new * C)[:, :1]), 0.0)
        shrink = jnp.exp2((old - new) * C)
        dls[...] = dls[...] * shrink + jnp.sum(p, axis=1, keepdims=True)
        gained = jnp.dot(
            p.astype(BF16), kvbuf[1, cc].reshape(CHUNK, HEAD_DIM), preferred_element_type=F32
        )
        dacc[...] = dacc[...] * shrink + gained
        return carry

    lax.fori_loop(0, 4, decode_visit, 0)
    first = lax.broadcasted_iota(jnp.int32, (32, HEAD_DIM), 1) < 64
    for i in range(4):
        rows = pl.ds(i * 32, 32)
        pmsg[i, 0] = dacc[rows, :]
        pmsg[i, 1] = jnp.where(first, dmx[rows, :], dls[rows, :])
    for i in range(4):
        slot = yhi * 2 + core
        to_tp(4 * z + i, pmsg.at[i], part.at[slot], part_send.at[i], part_recv.at[slot])

    for i in range(4):
        drain(part.at[i], part_recv.at[i])
    for i in range(3):
        drain(kvp.at[i], kvp_recv.at[i])
    step_key = rotate(kvp_own[0] + kvp[0, 0] + kvp[1, 0] + kvp[2, 0]).astype(BF16).astype(F32)
    step_value = (kvp_own[1] + kvp[0, 1] + kvp[1, 1] + kvp[2, 1]).astype(BF16).astype(F32)
    step_query = dq_own[...].astype(F32)
    here = jnp.sum(step_query * step_key, axis=1, keepdims=True)
    before = jnp.sum(step_query * pltpu.roll(step_key, 1, 0), axis=1, keepdims=True)
    later = lax.rem(lax.broadcasted_iota(jnp.int32, (32, 1), 0), 2) == 1
    before = jnp.where(later, before, NEG)
    tops = [part[i, 1][:, :1] for i in range(4)]
    sums = [part[i, 1][:, 64:65] for i in range(4)]
    top = jnp.maximum(here, before)
    for m in tops:
        top = jnp.maximum(top, m)
    p_here = jnp.exp2((here - top) * C)
    p_before = jnp.where(later, jnp.exp2((before - top) * C), 0.0)
    total = p_here + p_before
    mixed = p_here.astype(BF16).astype(F32) * step_value
    mixed = mixed + p_before.astype(BF16).astype(F32) * pltpu.roll(step_value, 1, 0)
    for i in range(4):
        w = jnp.exp2((tops[i] - top) * C)
        total = total + w * sums[i]
        mixed = mixed + w * part[i, 0]
    attended = (mixed / total).astype(BF16)
    half = wo_v.shape[1] // 2
    for i in range(2):
        opart[i] = jnp.dot(attended, wo_v[:, i * half : (i + 1) * half], preferred_element_type=F32)

    c = rcopy(opart.at[1 - core], rs0, rs0_send, rs0_recv, sibling)
    c.start()
    sends.append(c)
    drain(rs0, rs0_recv)
    hsum[...] = opart[core] + rs0[...]

    def slab(ref, n):
        rows = pl.ds(pl.multiple_of(lax.div(n, 4) * 8, 8), 8)
        return ref.at[rows, pl.ds(pl.multiple_of(lax.rem(n, 4) * 640, 128), 640)]

    mine = yhi * 8 + z
    for n in range(16):
        zz, yy = lax.rem(z + n % 8, 8), flip(yhi, n // 8)
        src = slab(hsum, yy * 8 + zz)
        if n:
            rcopy(src, rs.at[n], rs_send.at[n], rs_recv.at[n], dev(x, yy * 2 + ylo, zz, core)).start()
        else:
            pltpu.make_async_copy(src, rs.at[0], rs_recv.at[0]).start()
    for n in range(16):
        drain(rs.at[n], rs_recv.at[n])
    total_rows = rs[0]
    for n in range(1, 16):
        total_rows = total_rows + rs[n]
    rs[0] = total_rows
    for n in range(16):
        zz, yy = lax.rem(z + n % 8, 8), flip(yhi, n // 8)
        if n:
            rcopy(rs.at[0], slab(fbuf, mine), f_send.at[n], f_recv, dev(x, yy * 2 + ylo, zz, core)).start()
        else:
            pltpu.make_async_copy(rs.at[0], slab(fbuf, mine), f_recv).start()
    drain(fbuf, f_recv)
    c = rcopy(fbuf, fsib, fs_send, fs_recv, sibling)
    c.start()
    sends.append(c)
    drain(fsib, fs_recv)
    dec_ref[core] = fbuf[...].astype(BF16)
    dec_ref[1 - core] = fsib[...].astype(BF16)

    for n in range(1, 16):
        drain(rs.at[n], rs_send.at[n])
        drain(rs.at[n], f_send.at[n])
    for target, src, sem in late:
        pl.when(target != t)(lambda src=src, sem=sem: drain(src, sem))
    for i in range(3):
        drain(kvp_own, kvp_send.at[i])
    for kv in range(2):
        drain(kvbuf.at[0, pl.ds(0, 7), 0, 0], kv0_send.at[kv])
    drain(kvbuf.at[0, pl.ds(0, 15), 0, 0], q_send.at[0])
    drain(kvbuf.at[0, pl.ds(0, 16), 0, 0], q_send.at[1])
    drain(kvbuf.at[0, pl.ds(0, 15), 0, 0], o_send.at[0])
    drain(kvbuf.at[0, pl.ds(0, 16), 0, 0], o_send.at[1])
    for c in sends:
        c.wait_send()
    drain(out_ref, o_recv)


def shards(
    prompt_q, prompt_k, prompt_v, lengths, sample_states, norm_gain,
    w_query, b_query, w_key, b_key, w_value, b_value, w_out,
):
    samples, steps, width = sample_states.shape
    rows = samples * steps
    half_dim = HEAD_DIM // 2
    positions = (lengths[0] + jnp.arange(steps, dtype=jnp.int32)).astype(F32)[:, None]
    frequency = ROPE_BASE ** (-(2.0 * jnp.arange(half_dim, dtype=F32)) / HEAD_DIM)
    angles = positions * frequency
    cosine, sine = jnp.cos(angles), jnp.sin(angles)
    cosine = jnp.tile(jnp.concatenate([cosine, cosine], axis=1), (samples, 1))
    sine = jnp.tile(jnp.concatenate([-sine, sine], axis=1), (samples, 1))
    vmem = pl.BlockSpec(memory_space=pltpu.VMEM)
    smem = pl.BlockSpec(memory_space=pltpu.SMEM)
    hbm = pl.BlockSpec(memory_space=pl.ANY)
    dma = pltpu.SemaphoreType.DMA
    half = width // 2
    prefill, decoded = pl.pallas_call(
        kernel,
        out_shape=(
            jax.ShapeDtypeStruct(prompt_q.shape, BF16),
            jax.ShapeDtypeStruct((2, rows, half), BF16),
        ),
        in_specs=[hbm, hbm, hbm, vmem, vmem, vmem, vmem, smem, hbm, vmem, hbm, vmem, hbm, vmem, hbm],
        out_specs=(hbm, vmem),
        scratch_shapes=[
            pltpu.VMEM((2, 16, 8, 2, 64, HEAD_DIM), BF16),
            pltpu.VMEM((2, 8, 2, 64, HEAD_DIM), BF16),
            pltpu.VMEM((2, 8, 2, 64, HEAD_DIM), BF16),
            pltpu.VMEM((2, TILE, CHUNK), F32),
            pltpu.VMEM((2, CHUNK, HEAD_DIM), F32),
            pltpu.VMEM((2, CHUNK, HEAD_DIM), F32),
            pltpu.VMEM((2, CHUNK, HEAD_DIM), F32),
            pltpu.VMEM(w_query.shape, BF16),
            pltpu.VMEM(w_key.shape, BF16),
            pltpu.VMEM(w_value.shape, BF16),
            pltpu.VMEM(w_out.shape, BF16),
            pltpu.VMEM((rows, HEAD_DIM), BF16),
            pltpu.VMEM((4, rows, HEAD_DIM), BF16),
            pltpu.VMEM((2, rows, HEAD_DIM), F32),
            pltpu.VMEM((3, 2, rows, HEAD_DIM), F32),
            pltpu.VMEM((4, 2, rows, HEAD_DIM), F32),
            pltpu.VMEM((4, 2, rows, HEAD_DIM), F32),
            pltpu.VMEM((2, rows, half), F32),
            pltpu.VMEM((rows, half), F32),
            pltpu.VMEM((rows, half), F32),
            pltpu.VMEM((16, 8, 640), F32),
            pltpu.VMEM((rows, half), F32),
            pltpu.VMEM((rows, half), F32),
            pltpu.VMEM((4 * rows, HEAD_DIM), F32),
            pltpu.VMEM((4 * rows, HEAD_DIM), F32),
            pltpu.VMEM((4 * rows, HEAD_DIM), F32),
            dma((4,)),
            dma((2,)), dma((2,)), dma((2,)),
            dma((2,)), dma((2,)),
            dma((4, 4, 2)), dma((5, 4)), dma((4, 4)), dma((4, 4)),
            dma, dma((2,)),
            dma((4,)), dma((4,)),
            dma((3,)), dma((3,)),
            dma((4,)), dma((4,)),
            dma, dma, dma((16,)), dma((16,)), dma, dma((16,)), dma, dma,
        ],
        compiler_params=pltpu.CompilerParams(
            collective_id=0, has_side_effects=True, vmem_limit_bytes=56 * 2**20
        ),
    )(
        prompt_q, prompt_k, prompt_v, sample_states.reshape(rows, width), norm_gain[None],
        cosine, sine, lengths, w_query, b_query[None], w_key, b_key[None], w_value, b_value[None], w_out,
    )
    decode_out = jnp.concatenate([decoded[0], decoded[1]], axis=1).reshape(samples, steps, width)
    return prefill, decode_out


def solution(mesh):
    in_specs = (
        P(("grp", "tp"), None),
        P(("grp", "tp"), None),
        P(("grp", "tp"), None),
        P("grp"),
        P("grp", None, None),
        P(),
        P(None, "tp"),
        P("tp"),
        P(None, "tp"),
        P("tp"),
        P(None, "tp"),
        P("tp"),
        P("tp", None),
    )
    out_specs = (P(("grp", "tp"), None), P("grp", None, None))
    return jax.shard_map(shards, mesh=mesh, in_specs=in_specs, out_specs=out_specs, check_vma=False)
```

```python
import math

import jax
import jax.numpy as jnp
from jax import lax
from jax.experimental import pallas as pl
from jax.experimental.pallas import tpu as pltpu
from jax.sharding import PartitionSpec as P

HEADS = 32
KV_HEADS = 8
HEAD_DIM = 128
STEPS = 2
EPSILON = 1e-06
ROPE_BASE = 1000000.0
MESH = pl.DeviceIdType.MESH
F32 = jnp.float32
BF16 = jnp.bfloat16
NEG = -1e30
C = math.log2(math.e) / math.sqrt(HEAD_DIM)
NT = (((1,), (1,)), ((), ()))
CHUNK = 1024
TILE = 256


def dot_nt(a, b):
    return lax.dot_general(a, b, NT, preferred_element_type=F32)


def kernel(
    q_ref, k_ref, v_ref, st_ref, gain_ref, cos_ref, sin_ref, len_ref,
    wq_ref, bq_ref, wk_ref, bk_ref, wv_ref, bv_ref, wo_ref,
    out_ref, dec_ref,
    kvbuf, qbuf, obuf, S, acc, mx, ls,
    wq_v, wk_v, wv_v, wo_v, dq_own, dq, kvp_own, kvp, pmsg, part, opart, rs0, slabs, rs, fbuf, fsib,
    SD, stv, q_v, k_v, v_v,
    in_sem, w_sem, kv0_recv, kv0_loc, kv0_send, q_recv, q_send, ag_recv, ag_send, sib_recv, sib_send,
    o_recv, o_send, dq_recv, dq_send, kvp_recv, kvp_send, part_recv, part_send,
    rs0_recv, rs0_send, rs_recv, rs_send, f_recv, f_send, fs_recv, fs_send,
):
    g = lax.axis_index("grp")
    t = lax.axis_index("tp")
    x, ylo = lax.rem(g, 4), lax.div(g, 4)
    yhi, z, core = lax.div(t, 16), lax.rem(lax.div(t, 2), 8), lax.rem(t, 2)
    y = yhi * 2 + ylo
    own = (ylo * 4 + x) * 2 + yhi

    def dev(xx, yy, zz, cc):
        return {"grp": lax.rem(yy, 2) * 4 + xx, "tp": lax.div(yy, 2) * 16 + zz * 2 + cc}

    def flip(bit, by):
        return bit + by * (1 - 2 * bit)

    def column(by):
        return x + by * (3 - 2 * x), y + by * (3 - 2 * y)

    def rcopy(src, dst, send, recv, to):
        return pltpu.make_async_remote_copy(
            src_ref=src, dst_ref=dst, send_sem=send, recv_sem=recv, device_id=to, device_id_type=MESH
        )

    def drain(ref, sem):
        pltpu.make_async_copy(ref, ref, sem).wait()

    def head_cols(ref, h, width=HEAD_DIM):
        return ref.at[:, pl.ds(pl.multiple_of(h * width, width), width)]

    half = wo_v.shape[1] // 2

    loads = [
        pltpu.make_async_copy(a, b, in_sem.at[i])
        for i, (a, b) in enumerate(((k_ref, k_v), (v_ref, v_v), (q_ref, q_v)))
    ]
    for c in loads:
        c.start()
    weights = [
        pltpu.make_async_copy(a, b, w_sem.at[i])
        for i, (a, b) in enumerate(((wq_ref, wq_v), (wk_ref, wk_v), (wv_ref, wv_v), (wo_ref, wo_v)))
    ]
    for w in weights:
        w.start()

    barrier = pltpu.get_barrier_semaphore()

    def greet(to):
        pl.semaphore_signal(barrier, inc=1, device_id=to, device_id_type=MESH)

    y2 = lax.rem(y + 2, 4)
    for dc in range(2):
        for dz in range(8):
            zz, cc = lax.rem(z + dz, 8), flip(core, dc)
            if dz or dc:
                greet(dev(x, y, zz, cc))
            greet(dev(3 - x, 3 - y, zz, cc))
            greet(dev(x, y2, zz, cc))
    for d in (1, 3):
        greet(dev(lax.rem(x + d, 4), y, z, core))
        greet(dev(x, lax.rem(y + d, 4), z, core))
    for c in loads:
        c.wait()
    pl.semaphore_wait(barrier, 51)

    for dz in (4, 3, 5, 2, 6, 1, 7):
        zz = lax.rem(z + dz, 8)
        for kv, ref in enumerate((k_v, v_v)):
            rcopy(
                head_cols(ref, zz), kvbuf.at[kv, own, z, core], kv0_send.at[kv], kv0_recv.at[kv],
                dev(x, y, zz, core),
            ).start()
    kv_local = [
        pltpu.make_async_copy(head_cols(ref, z), kvbuf.at[kv, own, z, core], kv0_loc.at[kv])
        for kv, ref in enumerate((k_v, v_v))
    ]
    for c in kv_local:
        c.start()
    def send_queries(dp):
        px, py = column(dp)
        for dz in (4, 3, 5, 2, 6, 1, 7, 0):
            zz = lax.rem(z + dz, 8)
            for dc in range(2):
                cc = flip(core, dc)
                src = head_cols(q_v, 4 * zz + 2 * flip(ylo, dp) + cc)
                dst = qbuf.at[ylo, z, core]
                if dz or dp or dc:
                    rcopy(src, dst, q_send.at[dp], q_recv.at[ylo], dev(px, py, zz, cc)).start()
                else:
                    pltpu.make_async_copy(src, dst, q_recv.at[ylo]).start()

    send_queries(0)

    def place(o1, o2):
        ox, oy = (1 - core) * o1 + core * o2, core * o1 + (1 - core) * o2
        return lax.rem(x + ox, 4), lax.rem(y + oy, 4)

    def chunk_of(o1, o2):
        xx, yy = place(o1, o2)
        return (lax.rem(yy, 2) * 4 + xx) * 2 + lax.div(yy, 2)

    def block(o1, o2, kv=None):
        return kvbuf.at[slice(None) if kv is None else kv, chunk_of(o1, o2), :, core]

    def toward(axis, step):
        xx, yy = place(step, 0) if axis == 1 else place(0, step)
        return dev(xx, yy, z, core)

    def send(src, sem, recv, to):
        rcopy(src, src, sem, recv, to).start()

    sibling = dev(x, y, z, 1 - core)

    def to_sibling(o1, o2):
        send(block(o1, o2), sib_send.at[o1, o2], sib_recv.at[o1, o2], sibling)

    def from_sibling(o1, o2):
        drain(kvbuf.at[:, chunk_of(o1, o2), :, 1 - core], sib_recv.at[o2, o1])

    def open_axis1():
        send(block(0, 0), ag_send.at[0, 0], ag_recv.at[3, 0, 0], toward(1, 1))
        send(block(0, 0), ag_send.at[0, 1], ag_recv.at[1, 0, 0], toward(1, 3))

    def open_axis2(o1):
        send(block(o1, 0), ag_send.at[1 + o1, 0], ag_recv.at[o1, 3, 0], toward(2, 1))
        send(block(o1, 0), ag_send.at[1 + o1, 1], ag_recv.at[o1, 1, 0], toward(2, 3))

    def pass_axis1():
        drain(block(3, 0), ag_recv.at[3, 0, 0])
        send(block(3, 0, 0), ag_send.at[0, 2], ag_recv.at[2, 0, 0], toward(1, 1))
        drain(block(1, 0), ag_recv.at[1, 0, 0])
        send(block(1, 0, 1), ag_send.at[0, 3], ag_recv.at[2, 0, 1], toward(1, 3))

    def pass_axis2(o1):
        drain(block(o1, 3), ag_recv.at[o1, 3, 0])
        send(block(o1, 3, 0), ag_send.at[1 + o1, 2], ag_recv.at[o1, 2, 0], toward(2, 1))
        drain(block(o1, 1), ag_recv.at[o1, 1, 0])
        send(block(o1, 1, 1), ag_send.at[1 + o1, 3], ag_recv.at[o1, 2, 1], toward(2, 3))
        to_sibling(o1, 3)
        to_sibling(o1, 1)

    def end_axis(o1, o2):
        for kv in range(2):
            drain(block(o1, o2, kv), ag_recv.at[o1, o2, kv])
        to_sibling(o1, o2)

    for kv in range(2):
        kv_local[kv].wait()
        drain(kvbuf.at[kv, own, pl.ds(0, 7), core], kv0_recv.at[kv])
    open_axis1()
    open_axis2(0)
    to_sibling(0, 0)
    send_queries(1)

    for s in range(16):
        stv[pl.ds(2 * s, 2), :] = st_ref[s].astype(F32)
    states = stv[...]
    scale = lax.rsqrt(jnp.mean(states * states, axis=1, keepdims=True) + EPSILON)
    normed = jnp.concatenate(
        [
            (states[:, j * 128 : (j + 1) * 128] * scale * gain_ref[j : j + 1, :].astype(F32)).astype(BF16)
            for j in range(states.shape[1] // 128)
        ],
        axis=1,
    )
    for w in weights:
        w.wait()
    odd = lax.rem(lax.broadcasted_iota(jnp.int32, (32, HEAD_DIM), 0), 2) == 1
    cosine = jnp.concatenate([cos_ref[...], cos_ref[...]], axis=1)
    sine = jnp.concatenate([-sin_ref[...], sin_ref[...]], axis=1)
    cosine = jnp.where(odd, cosine[1:2, :], cosine[0:1, :])
    sine = jnp.where(odd, sine[1:2, :], sine[0:1, :])

    def rotate(value):
        return value * cosine + pltpu.roll(value, HEAD_DIM // 2, 1) * sine

    query = jnp.dot(normed, wq_v[...], preferred_element_type=F32) + bq_ref[...].astype(F32)
    dq_own[...] = rotate(query).astype(BF16)
    quarter = lax.rem(t, 4)
    spread = (
        lax.broadcasted_iota(jnp.int32, (32, HEAD_DIM), 1)
        == lax.broadcasted_iota(jnp.int32, (32, HEAD_DIM), 0) + quarter * 32
    ).astype(F32)
    for i, (w, b) in enumerate(((wk_v, bk_ref), (wv_v, bv_ref))):
        narrow = dot_nt(normed, w[...]) + b[...].astype(F32)
        kvp_own[i] = jnp.dot(narrow, spread, precision=lax.Precision.HIGHEST, preferred_element_type=F32)

    def to_tp(target, src, dst, send, recv):
        @pl.when(target != t)
        def _():
            rcopy(src, dst, send, recv, {"grp": g, "tp": target}).start()

        @pl.when(target == t)
        def _():
            pltpu.make_async_copy(src, dst, recv).start()

    for i in range(4):
        target = (i // 2) * 16 + lax.div(t, 4) * 2 + i % 2
        to_tp(target, dq_own, dq.at[quarter], dq_send.at[i], dq_recv.at[quarter])
    for m in range(1, 4):
        target = lax.div(t, 4) * 4 + lax.rem(quarter + m, 4)
        rcopy(kvp_own, kvp.at[m - 1], kvp_send.at[m - 1], kvp_recv.at[m - 1], {"grp": g, "tp": target}).start()

    acc[...] = jnp.zeros_like(acc)
    mx[...] = jnp.full_like(mx, NEG)
    ls[...] = jnp.zeros_like(ls)
    low = own + ylo * (15 - 2 * own)

    def unit(slot, cc, diagonal):
        tiles = CHUNK // TILE
        keys = kvbuf[0, cc].reshape(CHUNK, HEAD_DIM)
        values = kvbuf[1, cc].reshape(CHUNK, HEAD_DIM)
        held = {}

        def scores(i):
            width = (i + 1) * TILE if diagonal else CHUNK
            rows = pl.ds(i * TILE, TILE)
            s = dot_nt(qbuf[slot, 2 * i : 2 * i + 2].reshape(TILE, HEAD_DIM), keys[:width])
            if diagonal:
                r = lax.broadcasted_iota(jnp.int32, (TILE, width), 0) + i * TILE
                s = jnp.where(lax.broadcasted_iota(jnp.int32, (TILE, width), 1) <= r, s, NEG)
            S[i % 2, :, :width] = s
            old = mx[slot, rows, :]
            new = jnp.maximum(old, jnp.max(s, axis=1, keepdims=True))
            mx[slot, rows, :] = new
            held[i] = (old, new)

        def mix(i):
            width = (i + 1) * TILE if diagonal else CHUNK
            rows = pl.ds(i * TILE, TILE)
            old, new = held.pop(i)
            p = jnp.exp2(S[i % 2, :, :width] * C - (new * C)[:, :1])
            shrink = jnp.exp2((old - new) * C)
            ls[slot, rows, :] = ls[slot, rows, :] * shrink + jnp.sum(p, axis=1, keepdims=True)
            gained = jnp.dot(p.astype(BF16), values[:width], preferred_element_type=F32)
            acc[slot, rows, :] = acc[slot, rows, :] * shrink + gained

        scores(0)
        for i in range(tiles):
            if i + 1 < tiles:
                scores(i + 1)
            mix(i)

    def send_output(slot):
        obuf[slot] = (acc[slot] / ls[slot]).astype(BF16).reshape(8, 2, 64, HEAD_DIM)
        dp = flip(slot, ylo)
        px, py = column(dp)
        for dz in range(8):
            zz = lax.rem(z + dz, 8)
            for dc in range(2):
                cc = flip(core, dc)
                src = obuf.at[slot, zz, cc]
                dst = head_cols(out_ref, 4 * z + 2 * ylo + core)

                def away(src=src, dst=dst, to=dev(px, py, zz, cc), dp=dp):
                    rcopy(src, dst, o_send.at[dp], o_recv, to).start()

                if dz or dc:
                    away()
                else:
                    pl.when(dp == 1)(away)

                    @pl.when(dp == 0)
                    def _():
                        pltpu.make_async_copy(src, dst, o_recv).start()

    def decode_attend():
        for i in range(4):
            drain(dq.at[i], dq_recv.at[i])
        limit = len_ref[0]
        yq = lax.rem(y + core, 4)
        queries = dq[...].reshape(128, HEAD_DIM)
        chunks = [(lax.rem(yq, 2) * 4 + i) * 2 + lax.div(yq, 2) for i in range(4)]
        top = jnp.full((128, 1), NEG, F32)
        for i, cc in enumerate(chunks):
            s = dot_nt(queries, kvbuf[0, cc].reshape(CHUNK, HEAD_DIM))
            allowed = lax.broadcasted_iota(jnp.int32, (128, CHUNK), 1) + cc * CHUNK < limit
            s = jnp.where(allowed, s, NEG)
            SD[i] = s
            top = jnp.maximum(top, jnp.max(s, axis=1, keepdims=True))
        total = jnp.zeros((128, 1), F32)
        mixed = jnp.zeros((128, HEAD_DIM), F32)
        for i, cc in enumerate(chunks):
            s = SD[i]
            p = jnp.where(s > 0.5 * NEG, jnp.exp2(s * C - top * C), 0.0)
            total = total + jnp.sum(p, axis=1, keepdims=True)
            mixed = mixed + jnp.dot(
                p.astype(BF16), kvbuf[1, cc].reshape(CHUNK, HEAD_DIM), preferred_element_type=F32
            )
        first = lax.broadcasted_iota(jnp.int32, (32, HEAD_DIM), 1) < 64
        for i in range(4):
            rows = slice(i * 32, i * 32 + 32)
            pmsg[i, 0] = mixed[rows]
            pmsg[i, 1] = jnp.where(first, top[rows], total[rows])
        for i in range(4):
            slot = yhi * 2 + core
            to_tp(4 * z + i, pmsg.at[i], part.at[slot], part_send.at[i], part_recv.at[slot])

    def decode_join():
        for i in range(4):
            drain(part.at[i], part_recv.at[i])
        for i in range(3):
            drain(kvp.at[i], kvp_recv.at[i])
        step_key = rotate(kvp_own[0] + kvp[0, 0] + kvp[1, 0] + kvp[2, 0]).astype(BF16).astype(F32)
        step_value = (kvp_own[1] + kvp[0, 1] + kvp[1, 1] + kvp[2, 1]).astype(BF16).astype(F32)
        step_query = dq_own[...].astype(F32)
        here = jnp.sum(step_query * step_key, axis=1, keepdims=True)
        before = jnp.sum(step_query * pltpu.roll(step_key, 1, 0), axis=1, keepdims=True)
        later = lax.rem(lax.broadcasted_iota(jnp.int32, (32, 1), 0), 2) == 1
        before = jnp.where(later, before, NEG)
        tops = [part[i, 1][:, :1] for i in range(4)]
        sums = [part[i, 1][:, 64:65] for i in range(4)]
        top = jnp.maximum(here, before)
        for m in tops:
            top = jnp.maximum(top, m)
        p_here = jnp.exp2((here - top) * C)
        p_before = jnp.where(later, jnp.exp2((before - top) * C), 0.0)
        total = p_here + p_before
        mixed = p_here.astype(BF16).astype(F32) * step_value
        mixed = mixed + p_before.astype(BF16).astype(F32) * pltpu.roll(step_value, 1, 0)
        for i in range(4):
            w = jnp.exp2((tops[i] - top) * C)
            total = total + w * sums[i]
            mixed = mixed + w * part[i, 0]
        attended = (mixed / total).astype(BF16)
        for i in range(2):
            opart[i] = jnp.dot(attended, wo_v[:, i * half : (i + 1) * half], preferred_element_type=F32)
        rcopy(opart.at[1 - core], rs0, rs0_send, rs0_recv, sibling).start()

    mine = yhi * 8 + z

    def decode_sum():
        drain(rs0, rs0_recv)
        both = opart[core] + rs0[...]
        for n in range(16):
            rows, first = slice(n // 4 * 8, n // 4 * 8 + 8), n % 4 * 640
            pieces = [both[rows, first + j * 128 : first + j * 128 + 128] for j in range(5)]
            slabs[n] = jnp.concatenate(pieces + pieces[:1], axis=0).astype(BF16)
        for n in range(16):
            zz, yy = lax.rem(z + n % 8, 8), flip(yhi, n // 8)
            src = slabs.at[yy * 8 + zz]
            if n:
                rcopy(src, rs.at[n], rs_send.at[n], rs_recv.at[n], dev(x, yy * 2 + ylo, zz, core)).start()
            else:
                pltpu.make_async_copy(src, rs.at[0], rs_recv.at[0]).start()

    def decode_spread():
        for n in range(16):
            drain(rs.at[n], rs_recv.at[n])
        total_rows = rs[0].astype(F32)
        for n in range(1, 16):
            total_rows = total_rows + rs[n].astype(F32)
        slabs[mine] = total_rows.astype(BF16)
        for n in range(16):
            zz, yy = lax.rem(z + n % 8, 8), flip(yhi, n // 8)
            if n:
                rcopy(slabs.at[mine], fbuf.at[mine], f_send.at[n], f_recv, dev(x, yy * 2 + ylo, zz, core)).start()
            else:
                pltpu.make_async_copy(slabs.at[mine], fbuf.at[mine], f_recv).start()

    def decode_swap():
        drain(fbuf, f_recv)
        rcopy(fbuf, fsib, fs_send, fs_recv, sibling).start()

    def decode_finish():
        drain(fsib, fs_recv)
        here = lax.broadcasted_iota(jnp.int32, fbuf.shape[1:], 0) * 0 + core == 0
        for part_no in range(2):
            for group in range(4):
                pieces = []
                for n in range(4 * group, 4 * group + 4):
                    a, b = (fbuf, fsib) if part_no == 0 else (fsib, fbuf)
                    block_rows = jnp.where(here, a[n].astype(F32), b[n].astype(F32))
                    pieces += [block_rows[8 * j : 8 * j + 8] for j in range(5)]
                rows = jnp.concatenate(pieces, axis=1).astype(BF16)
                for r in range(4):
                    dec_ref[4 * group + r, :, part_no * half : (part_no + 1) * half] = rows[2 * r : 2 * r + 2]

    order = (
        (0, 0), (1, 0), (0, 1), (3, 0), (0, 3), (2, 0), (0, 2), (1, 1), (1, 3),
        (3, 1), (3, 3), (1, 2), (2, 1), (3, 2), (2, 3), (2, 2),
    )
    early = 9

    def look_up(table, v):
        found = v * 0 + table[0]
        for n in range(1, len(table)):
            found = jnp.where(v == n, table[n], found)
        return found

    def place_of(v):
        return look_up([o[0] for o in order], v), look_up([o[1] for o in order], v)

    def hop1():
        pass_axis1()
        open_axis2(1)
        open_axis2(3)
        to_sibling(1, 0)
        to_sibling(3, 0)
        pass_axis2(0)

    def hop2():
        end_axis(2, 0)
        open_axis2(2)

    def hop3():
        pass_axis2(1)
        pass_axis2(3)

    def hop4():
        end_axis(0, 2)

    def hop5():
        pass_axis2(2)

    def hop6():
        end_axis(1, 2)
        end_axis(3, 2)
        end_axis(2, 2)

    def item(i):
        second = i >= 16 + early
        slot = jnp.where(i < 2 * early, lax.rem(i, 2), jnp.where(second, 1, 0))
        v = jnp.where(i < 2 * early, lax.div(i, 2), jnp.where(second, i - 16, i - early))
        o1, o2 = place_of(v)
        return slot, v, o1, o2, chunk_of(o1, o2), low + slot * (15 - 2 * low)

    hops = ((2, hop2), (3, hop3), (3, hop4), (4, hop5), (5, hop6))
    steps = (
        (7, decode_attend), (9, decode_join), (10, decode_sum), (13, decode_spread), (16, decode_swap),
    )

    def work(u, carry):
        at, level, seen = carry

        def skips(i):
            slot, v, o1, o2, cc, last = item(i)
            return cc > last

        now = lax.while_loop(skips, lambda i: i + 1, at)
        slot, v, o1, o2, cc, last = item(now)
        due = look_up((1, 2, 2, 3, 3, 4, 4, 5), jnp.minimum(u, 7))
        due = jnp.maximum(due, jnp.where(v <= 4, 1, jnp.where(v <= 10, 3, 5)))
        for needs, hop in hops:
            pl.when((level < needs) & (needs <= due))(hop)
        known = jnp.where(u == 7, 16, jnp.maximum(seen, v + 1))

        def learn(n, c):
            from_sibling(*place_of(n))
            return c

        lax.fori_loop(seen, known, learn, 0)
        pl.when((at <= 16 + early) & (now >= 16 + early))(lambda: send_output(0))
        for when, step in steps:
            pl.when(u == when)(step)

        @pl.when(cc < last)
        def _():
            unit(slot, cc, False)

        @pl.when(cc == last)
        def _():
            unit(slot, cc, True)

        return now + 1, jnp.maximum(level, due), known

    drain(qbuf.at[ylo], q_recv.at[ylo])

    def all_work(u, carry):
        @pl.when(u == 1)
        def _():
            hop1()
            drain(qbuf.at[1 - ylo], q_recv.at[1 - ylo])

        return work(u, carry)

    zero = t * 0
    lax.fori_loop(0, 17, all_work, (zero, zero + 1, zero))
    send_output(1)
    decode_finish()

    for n in range(1, 16):
        drain(rs.at[n], rs_send.at[n])
        drain(rs.at[n], f_send.at[n])
    for i in range(4):
        pl.when((i // 2) * 16 + lax.div(t, 4) * 2 + i % 2 != t)(lambda i=i: drain(dq_own, dq_send.at[i]))
        pl.when(4 * z + i != t)(lambda i=i: drain(pmsg.at[i], part_send.at[i]))
    for i in range(3):
        drain(kvp_own, kvp_send.at[i])
    for kv in range(2):
        drain(kvbuf.at[0, pl.ds(0, 7), 0, 0], kv0_send.at[kv])
    drain(kvbuf.at[0, pl.ds(0, 15), 0, 0], q_send.at[0])
    drain(kvbuf.at[0, pl.ds(0, 16), 0, 0], q_send.at[1])
    drain(kvbuf.at[0, pl.ds(0, 15), 0, 0], o_send.at[0])
    drain(kvbuf.at[0, pl.ds(0, 16), 0, 0], o_send.at[1])
    whole, half_block = kvbuf.at[:, 0, :, 0], kvbuf.at[0, 0, :, 0]
    for a in range(5):
        for b in range(4):
            drain(whole if b < 2 else half_block, ag_send.at[a, b])
    for o1 in range(4):
        for o2 in range(4):
            drain(whole, sib_send.at[o1, o2])
    drain(rs0, rs0_send)
    drain(fbuf, fs_send)
    drain(out_ref, o_recv)


def hand_over(a_ref, b_ref, out_ref, dec_ref):
    out_ref[...] = a_ref[...]
    dec_ref[...] = b_ref[...]


def shards(
    prompt_q, prompt_k, prompt_v, lengths, sample_states, norm_gain,
    w_query, b_query, w_key, b_key, w_value, b_value, w_out,
):
    samples, steps, width = sample_states.shape
    rows = samples * steps
    half_dim = HEAD_DIM // 2
    positions = (lengths[0] + jnp.arange(steps, dtype=jnp.int32)).astype(F32)[:, None]
    frequency = ROPE_BASE ** (-(2.0 * jnp.arange(half_dim, dtype=F32)) / HEAD_DIM)
    angles = positions * frequency
    cosine, sine = jnp.cos(angles), jnp.sin(angles)
    vmem = pl.BlockSpec(memory_space=pltpu.VMEM)
    smem = pl.BlockSpec(memory_space=pltpu.SMEM)
    hbm = pl.BlockSpec(memory_space=pl.ANY)
    dma = pltpu.SemaphoreType.DMA
    half = width // 2
    prefill, decoded = pl.pallas_call(
        kernel,
        out_shape=(
            jax.ShapeDtypeStruct(prompt_q.shape, BF16),
            jax.ShapeDtypeStruct(sample_states.shape, BF16),
        ),
        in_specs=[hbm, hbm, hbm, vmem, vmem, vmem, vmem, smem, hbm, vmem, hbm, vmem, hbm, vmem, hbm],
        out_specs=(vmem, vmem),
        scratch_shapes=[
            pltpu.VMEM((2, 16, 8, 2, 64, HEAD_DIM), BF16),
            pltpu.VMEM((2, 8, 2, 64, HEAD_DIM), BF16),
            pltpu.VMEM((2, 8, 2, 64, HEAD_DIM), BF16),
            pltpu.VMEM((2, TILE, CHUNK), F32),
            pltpu.VMEM((2, CHUNK, HEAD_DIM), F32),
            pltpu.VMEM((2, CHUNK, HEAD_DIM), F32),
            pltpu.VMEM((2, CHUNK, HEAD_DIM), F32),
            pltpu.VMEM(w_query.shape, BF16),
            pltpu.VMEM(w_key.shape[::-1], BF16),
            pltpu.VMEM(w_value.shape[::-1], BF16),
            pltpu.VMEM(w_out.shape, BF16),
            pltpu.VMEM((rows, HEAD_DIM), BF16),
            pltpu.VMEM((4, rows, HEAD_DIM), BF16),
            pltpu.VMEM((2, rows, HEAD_DIM), F32),
            pltpu.VMEM((3, 2, rows, HEAD_DIM), F32),
            pltpu.VMEM((4, 2, rows, HEAD_DIM), F32),
            pltpu.VMEM((4, 2, rows, HEAD_DIM), F32),
            pltpu.VMEM((2, rows, half), F32),
            pltpu.VMEM((rows, half), F32),
            pltpu.VMEM((16, 48, HEAD_DIM), BF16),
            pltpu.VMEM((16, 48, HEAD_DIM), BF16),
            pltpu.VMEM((16, 48, HEAD_DIM), BF16),
            pltpu.VMEM((16, 48, HEAD_DIM), BF16),
            pltpu.VMEM((4, 4 * rows, CHUNK), F32),
            pltpu.VMEM((rows, width), F32),
            pltpu.VMEM(prompt_q.shape, BF16),
            pltpu.VMEM(prompt_k.shape, BF16),
            pltpu.VMEM(prompt_v.shape, BF16),
            dma((3,)),
            dma((4,)),
            dma((2,)), dma((2,)), dma((2,)),
            dma((2,)), dma((2,)),
            dma((4, 4, 2)), dma((5, 4)), dma((4, 4)), dma((4, 4)),
            dma, dma((2,)),
            dma((4,)), dma((4,)),
            dma((3,)), dma((3,)),
            dma((4,)), dma((4,)),
            dma, dma, dma((16,)), dma((16,)), dma, dma((16,)), dma, dma,
        ],
        compiler_params=pltpu.CompilerParams(
            collective_id=0, has_side_effects=True, vmem_limit_bytes=56 * 2**20
        ),
    )(
        prompt_q, prompt_k, prompt_v, sample_states, norm_gain.reshape(-1, 128),
        cosine, sine, lengths, w_query, b_query[None], w_key.T, b_key[None],
        w_value.T, b_value[None], w_out,
    )
    return pl.pallas_call(
        hand_over,
        out_shape=(
            jax.ShapeDtypeStruct(prefill.shape, BF16),
            jax.ShapeDtypeStruct(decoded.shape, BF16),
        ),
        in_specs=[vmem, vmem],
        out_specs=(vmem, vmem),
    )(prefill, decoded)


def solution(mesh):
    in_specs = (
        P(("grp", "tp"), None),
        P(("grp", "tp"), None),
        P(("grp", "tp"), None),
        P("grp"),
        P("grp", None, None),
        P(),
        P(None, "tp"),
        P("tp"),
        P(None, "tp"),
        P("tp"),
        P(None, "tp"),
        P("tp"),
        P("tp", None),
    )
    out_specs = (P(("grp", "tp"), None), P("grp", None, None))
    return jax.shard_map(shards, mesh=mesh, in_specs=in_specs, out_specs=out_specs, check_vma=False)
```

```python
import math

import jax
import jax.numpy as jnp
from jax import lax
from jax.experimental import pallas as pl
from jax.experimental.pallas import tpu as pltpu
from jax.sharding import PartitionSpec as P

HEADS = 32
KV_HEADS = 8
HEAD_DIM = 128
STEPS = 2
EPSILON = 1e-06
ROPE_BASE = 1000000.0
MESH = pl.DeviceIdType.MESH
F32 = jnp.float32
BF16 = jnp.bfloat16
NEG = -1e30
C = math.log2(math.e) / math.sqrt(HEAD_DIM)
NT = (((1,), (1,)), ((), ()))
CHUNK = 1024
TILE = 256


def dot_nt(a, b):
    return lax.dot_general(a, b, NT, preferred_element_type=F32)


def kernel(
    q_ref, k_ref, v_ref, st_ref, gain_ref, cos_ref, sin_ref, len_ref,
    wq_ref, bq_ref, wk_ref, bk_ref, wv_ref, bv_ref, wo_ref,
    out_ref, dec_ref,
    kvbuf, qbuf, obuf, S, acc, mx, ls,
    wq_v, wk_v, wv_v, wo_v, dq_own, dq, kvp_own, kvp, pmsg, part, opart, rs0, slabs, rs, fbuf, fsib,
    SD, stv, q_v, k_v, v_v,
    in_sem, w_sem, kv0_recv, kv0_loc, kv0_send, q_recv, q_send, ag_recv, ag_send, sib_recv, sib_send,
    o_recv, o_send, dq_recv, dq_send, kvp_recv, kvp_send, part_recv, part_send,
    rs0_recv, rs0_send, rs_recv, rs_send, f_recv, f_send, fs_recv, fs_send,
):
    g = lax.axis_index("grp")
    t = lax.axis_index("tp")
    x, ylo = lax.rem(g, 4), lax.div(g, 4)
    yhi, z, core = lax.div(t, 16), lax.rem(lax.div(t, 2), 8), lax.rem(t, 2)
    y = yhi * 2 + ylo
    own = (ylo * 4 + x) * 2 + yhi

    def dev(xx, yy, zz, cc):
        return {"grp": lax.rem(yy, 2) * 4 + xx, "tp": lax.div(yy, 2) * 16 + zz * 2 + cc}

    def flip(bit, by):
        return bit + by * (1 - 2 * bit)

    def column(by):
        return x + by * (3 - 2 * x), y + by * (3 - 2 * y)

    def rcopy(src, dst, send, recv, to):
        return pltpu.make_async_remote_copy(
            src_ref=src, dst_ref=dst, send_sem=send, recv_sem=recv, device_id=to, device_id_type=MESH
        )

    def drain(ref, sem):
        pltpu.make_async_copy(ref, ref, sem).wait()

    def head_cols(ref, h, width=HEAD_DIM):
        return ref.at[:, pl.ds(pl.multiple_of(h * width, width), width)]

    half = wo_v.shape[1] // 2

    loads = [
        pltpu.make_async_copy(a, b, in_sem.at[i])
        for i, (a, b) in enumerate(((k_ref, k_v), (v_ref, v_v), (q_ref, q_v)))
    ]
    for c in loads:
        c.start()
    weights = [
        pltpu.make_async_copy(a, b, w_sem.at[i])
        for i, (a, b) in enumerate(((wq_ref, wq_v), (wk_ref, wk_v), (wv_ref, wv_v), (wo_ref, wo_v)))
    ]
    for w in weights:
        w.start()

    barrier = pltpu.get_barrier_semaphore()

    def greet(to):
        pl.semaphore_signal(barrier, inc=1, device_id=to, device_id_type=MESH)

    y2 = lax.rem(y + 2, 4)
    for dc in range(2):
        for dz in range(8):
            zz, cc = lax.rem(z + dz, 8), flip(core, dc)
            if dz or dc:
                greet(dev(x, y, zz, cc))
            greet(dev(3 - x, 3 - y, zz, cc))
            greet(dev(x, y2, zz, cc))
    for d in (1, 3):
        greet(dev(lax.rem(x + d, 4), y, z, core))
        greet(dev(x, lax.rem(y + d, 4), z, core))
    for c in loads:
        c.wait()
    pl.semaphore_wait(barrier, 51)

    for dz in (4, 3, 5, 2, 6, 1, 7):
        zz = lax.rem(z + dz, 8)
        for kv, ref in enumerate((k_v, v_v)):
            rcopy(
                head_cols(ref, zz), kvbuf.at[kv, own, z, core], kv0_send.at[kv], kv0_recv.at[kv],
                dev(x, y, zz, core),
            ).start()
    kv_local = [
        pltpu.make_async_copy(head_cols(ref, z), kvbuf.at[kv, own, z, core], kv0_loc.at[kv])
        for kv, ref in enumerate((k_v, v_v))
    ]
    for c in kv_local:
        c.start()
    def send_queries(dp):
        px, py = column(dp)
        for dz in (4, 3, 5, 2, 6, 1, 7, 0):
            zz = lax.rem(z + dz, 8)
            for dc in range(2):
                cc = flip(core, dc)
                src = head_cols(q_v, 4 * zz + 2 * flip(ylo, dp) + cc)
                dst = qbuf.at[ylo, z, core]
                if dz or dp or dc:
                    rcopy(src, dst, q_send.at[dp], q_recv.at[ylo], dev(px, py, zz, cc)).start()
                else:
                    pltpu.make_async_copy(src, dst, q_recv.at[ylo]).start()

    send_queries(0)

    for s in range(16):
        stv[pl.ds(2 * s, 2), :] = st_ref[s].astype(F32)
    states = stv[...]
    scale = lax.rsqrt(jnp.mean(states * states, axis=1, keepdims=True) + EPSILON)
    normed = jnp.concatenate(
        [
            (states[:, j * 128 : (j + 1) * 128] * scale * gain_ref[j : j + 1, :].astype(F32)).astype(BF16)
            for j in range(states.shape[1] // 128)
        ],
        axis=1,
    )
    for w in weights:
        w.wait()
    odd = lax.rem(lax.broadcasted_iota(jnp.int32, (32, HEAD_DIM), 0), 2) == 1
    cosine = jnp.concatenate([cos_ref[...], cos_ref[...]], axis=1)
    sine = jnp.concatenate([-sin_ref[...], sin_ref[...]], axis=1)
    cosine = jnp.where(odd, cosine[1:2, :], cosine[0:1, :])
    sine = jnp.where(odd, sine[1:2, :], sine[0:1, :])

    def rotate(value):
        return value * cosine + pltpu.roll(value, HEAD_DIM // 2, 1) * sine

    query = jnp.dot(normed, wq_v[...], preferred_element_type=F32) + bq_ref[...].astype(F32)
    dq_own[...] = rotate(query).astype(BF16)
    quarter = lax.rem(t, 4)
    spread = (
        lax.broadcasted_iota(jnp.int32, (32, HEAD_DIM), 1)
        == lax.broadcasted_iota(jnp.int32, (32, HEAD_DIM), 0) + quarter * 32
    ).astype(F32)
    for i, (w, b) in enumerate(((wk_v, bk_ref), (wv_v, bv_ref))):
        narrow = dot_nt(normed, w[...]) + b[...].astype(F32)
        kvp_own[i] = jnp.dot(narrow, spread, precision=lax.Precision.HIGHEST, preferred_element_type=F32)

    def to_tp(target, src, dst, send, recv):
        @pl.when(target != t)
        def _():
            rcopy(src, dst, send, recv, {"grp": g, "tp": target}).start()

        @pl.when(target == t)
        def _():
            pltpu.make_async_copy(src, dst, recv).start()

    for i in range(4):
        target = (i // 2) * 16 + lax.div(t, 4) * 2 + i % 2
        to_tp(target, dq_own, dq.at[quarter], dq_send.at[i], dq_recv.at[quarter])
    for m in range(1, 4):
        target = lax.div(t, 4) * 4 + lax.rem(quarter + m, 4)
        rcopy(kvp_own, kvp.at[m - 1], kvp_send.at[m - 1], kvp_recv.at[m - 1], {"grp": g, "tp": target}).start()

    acc[...] = jnp.zeros_like(acc)
    mx[...] = jnp.full_like(mx, NEG)
    ls[...] = jnp.zeros_like(ls)

    def place(o1, o2):
        ox, oy = (1 - core) * o1 + core * o2, core * o1 + (1 - core) * o2
        return lax.rem(x + ox, 4), lax.rem(y + oy, 4)

    def chunk_of(o1, o2):
        xx, yy = place(o1, o2)
        return (lax.rem(yy, 2) * 4 + xx) * 2 + lax.div(yy, 2)

    def block(o1, o2, kv=None):
        return kvbuf.at[slice(None) if kv is None else kv, chunk_of(o1, o2), :, core]

    def toward(axis, step):
        xx, yy = place(step, 0) if axis == 1 else place(0, step)
        return dev(xx, yy, z, core)

    def send(src, sem, recv, to):
        rcopy(src, src, sem, recv, to).start()

    sibling = dev(x, y, z, 1 - core)

    def to_sibling(o1, o2):
        send(block(o1, o2), sib_send.at[o1, o2], sib_recv.at[o1, o2], sibling)

    def from_sibling(o1, o2):
        drain(kvbuf.at[:, chunk_of(o1, o2), :, 1 - core], sib_recv.at[o2, o1])

    def open_axis1():
        send(block(0, 0), ag_send.at[0, 0], ag_recv.at[3, 0, 0], toward(1, 1))
        send(block(0, 0), ag_send.at[0, 1], ag_recv.at[1, 0, 0], toward(1, 3))

    def open_axis2(o1):
        send(block(o1, 0), ag_send.at[1 + o1, 0], ag_recv.at[o1, 3, 0], toward(2, 1))
        send(block(o1, 0), ag_send.at[1 + o1, 1], ag_recv.at[o1, 1, 0], toward(2, 3))

    def pass_axis1():
        drain(block(3, 0), ag_recv.at[3, 0, 0])
        send(block(3, 0, 0), ag_send.at[0, 2], ag_recv.at[2, 0, 0], toward(1, 1))
        drain(block(1, 0), ag_recv.at[1, 0, 0])
        send(block(1, 0, 1), ag_send.at[0, 3], ag_recv.at[2, 0, 1], toward(1, 3))

    def pass_axis2(o1):
        drain(block(o1, 3), ag_recv.at[o1, 3, 0])
        send(block(o1, 3, 0), ag_send.at[1 + o1, 2], ag_recv.at[o1, 2, 0], toward(2, 1))
        drain(block(o1, 1), ag_recv.at[o1, 1, 0])
        send(block(o1, 1, 1), ag_send.at[1 + o1, 3], ag_recv.at[o1, 2, 1], toward(2, 3))
        to_sibling(o1, 3)
        to_sibling(o1, 1)

    def end_axis(o1, o2):
        for kv in range(2):
            drain(block(o1, o2, kv), ag_recv.at[o1, o2, kv])
        to_sibling(o1, o2)

    for kv in range(2):
        kv_local[kv].wait()
        drain(kvbuf.at[kv, own, pl.ds(0, 7), core], kv0_recv.at[kv])
    open_axis1()
    open_axis2(0)
    to_sibling(0, 0)
    send_queries(1)

    low = own + ylo * (15 - 2 * own)

    def unit(slot, cc, diagonal):
        tiles = CHUNK // TILE
        keys = kvbuf[0, cc].reshape(CHUNK, HEAD_DIM)
        values = kvbuf[1, cc].reshape(CHUNK, HEAD_DIM)
        held = {}

        def scores(i):
            width = (i + 1) * TILE if diagonal else CHUNK
            rows = pl.ds(i * TILE, TILE)
            s = dot_nt(qbuf[slot, 2 * i : 2 * i + 2].reshape(TILE, HEAD_DIM), keys[:width])
            if diagonal:
                r = lax.broadcasted_iota(jnp.int32, (TILE, width), 0) + i * TILE
                s = jnp.where(lax.broadcasted_iota(jnp.int32, (TILE, width), 1) <= r, s, NEG)
            S[i % 2, :, :width] = s
            old = mx[slot, rows, :]
            new = jnp.maximum(old, jnp.max(s, axis=1, keepdims=True))
            mx[slot, rows, :] = new
            held[i] = (old, new)

        def mix(i):
            width = (i + 1) * TILE if diagonal else CHUNK
            rows = pl.ds(i * TILE, TILE)
            old, new = held.pop(i)
            p = jnp.exp2(S[i % 2, :, :width] * C - (new * C)[:, :1])
            shrink = jnp.exp2((old - new) * C)
            ls[slot, rows, :] = ls[slot, rows, :] * shrink + jnp.sum(p, axis=1, keepdims=True)
            gained = jnp.dot(p.astype(BF16), values[:width], preferred_element_type=F32)
            acc[slot, rows, :] = acc[slot, rows, :] * shrink + gained

        scores(0)
        for i in range(tiles):
            if i + 1 < tiles:
                scores(i + 1)
            mix(i)

    def send_output(slot):
        obuf[slot] = (acc[slot] / ls[slot]).astype(BF16).reshape(8, 2, 64, HEAD_DIM)
        dp = flip(slot, ylo)
        px, py = column(dp)
        for dz in range(8):
            zz = lax.rem(z + dz, 8)
            for dc in range(2):
                cc = flip(core, dc)
                src = obuf.at[slot, zz, cc]
                dst = head_cols(out_ref, 4 * z + 2 * ylo + core)

                def away(src=src, dst=dst, to=dev(px, py, zz, cc), dp=dp):
                    rcopy(src, dst, o_send.at[dp], o_recv, to).start()

                if dz or dc:
                    away()
                else:
                    pl.when(dp == 1)(away)

                    @pl.when(dp == 0)
                    def _():
                        pltpu.make_async_copy(src, dst, o_recv).start()

    def decode_attend():
        for i in range(4):
            drain(dq.at[i], dq_recv.at[i])
        limit = len_ref[0]
        yq = lax.rem(y + core, 4)
        queries = dq[...].reshape(128, HEAD_DIM)
        chunks = [(lax.rem(yq, 2) * 4 + i) * 2 + lax.div(yq, 2) for i in range(4)]
        top = jnp.full((128, 1), NEG, F32)
        for i, cc in enumerate(chunks):
            s = dot_nt(queries, kvbuf[0, cc].reshape(CHUNK, HEAD_DIM))
            allowed = lax.broadcasted_iota(jnp.int32, (128, CHUNK), 1) + cc * CHUNK < limit
            s = jnp.where(allowed, s, NEG)
            SD[i] = s
            top = jnp.maximum(top, jnp.max(s, axis=1, keepdims=True))
        total = jnp.zeros((128, 1), F32)
        mixed = jnp.zeros((128, HEAD_DIM), F32)
        for i, cc in enumerate(chunks):
            s = SD[i]
            p = jnp.where(s > 0.5 * NEG, jnp.exp2(s * C - top * C), 0.0)
            total = total + jnp.sum(p, axis=1, keepdims=True)
            mixed = mixed + jnp.dot(
                p.astype(BF16), kvbuf[1, cc].reshape(CHUNK, HEAD_DIM), preferred_element_type=F32
            )
        first = lax.broadcasted_iota(jnp.int32, (32, HEAD_DIM), 1) < 64
        for i in range(4):
            rows = slice(i * 32, i * 32 + 32)
            pmsg[i, 0] = mixed[rows]
            pmsg[i, 1] = jnp.where(first, top[rows], total[rows])
        for i in range(4):
            slot = yhi * 2 + core
            to_tp(4 * z + i, pmsg.at[i], part.at[slot], part_send.at[i], part_recv.at[slot])

    def decode_join():
        for i in range(4):
            drain(part.at[i], part_recv.at[i])
        for i in range(3):
            drain(kvp.at[i], kvp_recv.at[i])
        step_key = rotate(kvp_own[0] + kvp[0, 0] + kvp[1, 0] + kvp[2, 0]).astype(BF16).astype(F32)
        step_value = (kvp_own[1] + kvp[0, 1] + kvp[1, 1] + kvp[2, 1]).astype(BF16).astype(F32)
        step_query = dq_own[...].astype(F32)
        here = jnp.sum(step_query * step_key, axis=1, keepdims=True)
        before = jnp.sum(step_query * pltpu.roll(step_key, 1, 0), axis=1, keepdims=True)
        later = lax.rem(lax.broadcasted_iota(jnp.int32, (32, 1), 0), 2) == 1
        before = jnp.where(later, before, NEG)
        tops = [part[i, 1][:, :1] for i in range(4)]
        sums = [part[i, 1][:, 64:65] for i in range(4)]
        top = jnp.maximum(here, before)
        for m in tops:
            top = jnp.maximum(top, m)
        p_here = jnp.exp2((here - top) * C)
        p_before = jnp.where(later, jnp.exp2((before - top) * C), 0.0)
        total = p_here + p_before
        mixed = p_here.astype(BF16).astype(F32) * step_value
        mixed = mixed + p_before.astype(BF16).astype(F32) * pltpu.roll(step_value, 1, 0)
        for i in range(4):
            w = jnp.exp2((tops[i] - top) * C)
            total = total + w * sums[i]
            mixed = mixed + w * part[i, 0]
        attended = (mixed / total).astype(BF16)
        for i in range(2):
            opart[i] = jnp.dot(attended, wo_v[:, i * half : (i + 1) * half], preferred_element_type=F32)
        rcopy(opart.at[1 - core], rs0, rs0_send, rs0_recv, sibling).start()

    mine = yhi * 8 + z

    def decode_sum():
        drain(rs0, rs0_recv)
        both = opart[core] + rs0[...]
        for n in range(16):
            rows, first = slice(n // 4 * 8, n // 4 * 8 + 8), n % 4 * 640
            pieces = [both[rows, first + j * 128 : first + j * 128 + 128] for j in range(5)]
            slabs[n] = jnp.concatenate(pieces + pieces[:1], axis=0).astype(BF16)
        for n in range(16):
            zz, yy = lax.rem(z + n % 8, 8), flip(yhi, n // 8)
            src = slabs.at[yy * 8 + zz]
            if n:
                rcopy(src, rs.at[n], rs_send.at[n], rs_recv.at[n], dev(x, yy * 2 + ylo, zz, core)).start()
            else:
                pltpu.make_async_copy(src, rs.at[0], rs_recv.at[0]).start()

    def decode_spread():
        for n in range(16):
            drain(rs.at[n], rs_recv.at[n])
        total_rows = rs[0].astype(F32)
        for n in range(1, 16):
            total_rows = total_rows + rs[n].astype(F32)
        slabs[mine] = total_rows.astype(BF16)
        for n in range(16):
            zz, yy = lax.rem(z + n % 8, 8), flip(yhi, n // 8)
            if n:
                rcopy(slabs.at[mine], fbuf.at[mine], f_send.at[n], f_recv, dev(x, yy * 2 + ylo, zz, core)).start()
            else:
                pltpu.make_async_copy(slabs.at[mine], fbuf.at[mine], f_recv).start()

    def decode_swap():
        drain(fbuf, f_recv)
        rcopy(fbuf, fsib, fs_send, fs_recv, sibling).start()

    def decode_finish():
        drain(fsib, fs_recv)
        here = lax.broadcasted_iota(jnp.int32, fbuf.shape[1:], 0) * 0 + core == 0
        for part_no in range(2):
            for group in range(4):
                pieces = []
                for n in range(4 * group, 4 * group + 4):
                    a, b = (fbuf, fsib) if part_no == 0 else (fsib, fbuf)
                    block_rows = jnp.where(here, a[n].astype(F32), b[n].astype(F32))
                    pieces += [block_rows[8 * j : 8 * j + 8] for j in range(5)]
                rows = jnp.concatenate(pieces, axis=1).astype(BF16)
                for r in range(4):
                    dec_ref[4 * group + r, :, part_no * half : (part_no + 1) * half] = rows[2 * r : 2 * r + 2]

    order = (
        (0, 0), (1, 0), (0, 1), (3, 0), (0, 3), (2, 0), (0, 2), (1, 1), (1, 3),
        (3, 1), (3, 3), (1, 2), (2, 1), (3, 2), (2, 3), (2, 2),
    )
    early = 9

    def look_up(table, v):
        found = v * 0 + table[0]
        for n in range(1, len(table)):
            found = jnp.where(v == n, table[n], found)
        return found

    def place_of(v):
        return look_up([o[0] for o in order], v), look_up([o[1] for o in order], v)

    def hop1():
        pass_axis1()
        open_axis2(1)
        open_axis2(3)
        to_sibling(1, 0)
        to_sibling(3, 0)
        pass_axis2(0)

    def hop2():
        end_axis(2, 0)
        open_axis2(2)

    def hop3():
        pass_axis2(1)
        pass_axis2(3)

    def hop4():
        end_axis(0, 2)

    def hop5():
        pass_axis2(2)

    def hop6():
        end_axis(1, 2)
        end_axis(3, 2)
        end_axis(2, 2)

    def item(i):
        second = i >= 16 + early
        slot = jnp.where(i < 2 * early, lax.rem(i, 2), jnp.where(second, 1, 0))
        v = jnp.where(i < 2 * early, lax.div(i, 2), jnp.where(second, i - 16, i - early))
        o1, o2 = place_of(v)
        return slot, v, o1, o2, chunk_of(o1, o2), low + slot * (15 - 2 * low)

    hops = ((2, hop2), (3, hop3), (3, hop4), (4, hop5), (5, hop6))
    steps = (
        (6, decode_attend), (8, decode_join), (9, decode_sum), (12, decode_spread), (16, decode_swap),
    )

    def work(u, carry):
        at, level, seen = carry

        def skips(i):
            slot, v, o1, o2, cc, last = item(i)
            return cc > last

        now = lax.while_loop(skips, lambda i: i + 1, at)
        slot, v, o1, o2, cc, last = item(now)
        due = look_up((1, 2, 2, 3, 3, 4, 5), jnp.minimum(u, 6))
        due = jnp.maximum(due, jnp.where(v <= 4, 1, jnp.where(v <= 10, 3, 5)))
        for needs, hop in hops:
            pl.when((level < needs) & (needs <= due))(hop)
        known = jnp.where(u == 6, 16, jnp.maximum(seen, v + 1))

        def learn(n, c):
            from_sibling(*place_of(n))
            return c

        lax.fori_loop(seen, known, learn, 0)
        pl.when((at <= 16 + early) & (now >= 16 + early))(lambda: send_output(0))
        for when, step in steps:
            pl.when(u == when)(step)

        @pl.when(cc < last)
        def _():
            unit(slot, cc, False)

        @pl.when(cc == last)
        def _():
            unit(slot, cc, True)

        return now + 1, jnp.maximum(level, due), known

    drain(qbuf.at[ylo], q_recv.at[ylo])

    def all_work(u, carry):
        @pl.when(u == 1)
        def _():
            hop1()
            drain(qbuf.at[1 - ylo], q_recv.at[1 - ylo])

        return work(u, carry)

    zero = t * 0
    lax.fori_loop(0, 17, all_work, (zero, zero + 1, zero))
    send_output(1)
    decode_finish()

    for n in range(1, 16):
        drain(rs.at[n], rs_send.at[n])
        drain(rs.at[n], f_send.at[n])
    for i in range(4):
        pl.when((i // 2) * 16 + lax.div(t, 4) * 2 + i % 2 != t)(lambda i=i: drain(dq_own, dq_send.at[i]))
        pl.when(4 * z + i != t)(lambda i=i: drain(pmsg.at[i], part_send.at[i]))
    for i in range(3):
        drain(kvp_own, kvp_send.at[i])
    for kv in range(2):
        drain(kvbuf.at[0, pl.ds(0, 7), 0, 0], kv0_send.at[kv])
    drain(kvbuf.at[0, pl.ds(0, 15), 0, 0], q_send.at[0])
    drain(kvbuf.at[0, pl.ds(0, 16), 0, 0], q_send.at[1])
    drain(kvbuf.at[0, pl.ds(0, 15), 0, 0], o_send.at[0])
    drain(kvbuf.at[0, pl.ds(0, 16), 0, 0], o_send.at[1])
    whole, half_block = kvbuf.at[:, 0, :, 0], kvbuf.at[0, 0, :, 0]
    for a in range(5):
        for b in range(4):
            drain(whole if b < 2 else half_block, ag_send.at[a, b])
    for o1 in range(4):
        for o2 in range(4):
            drain(whole, sib_send.at[o1, o2])
    drain(rs0, rs0_send)
    drain(fbuf, fs_send)
    drain(out_ref, o_recv)


def hand_over(a_ref, b_ref, out_ref, dec_ref):
    out_ref[...] = a_ref[...]
    dec_ref[...] = b_ref[...]


def shards(
    prompt_q, prompt_k, prompt_v, lengths, sample_states, norm_gain,
    w_query, b_query, w_key, b_key, w_value, b_value, w_out,
):
    samples, steps, width = sample_states.shape
    rows = samples * steps
    half_dim = HEAD_DIM // 2
    positions = (lengths[0] + jnp.arange(steps, dtype=jnp.int32)).astype(F32)[:, None]
    frequency = ROPE_BASE ** (-(2.0 * jnp.arange(half_dim, dtype=F32)) / HEAD_DIM)
    angles = positions * frequency
    cosine, sine = jnp.cos(angles), jnp.sin(angles)
    vmem = pl.BlockSpec(memory_space=pltpu.VMEM)
    smem = pl.BlockSpec(memory_space=pltpu.SMEM)
    hbm = pl.BlockSpec(memory_space=pl.ANY)
    dma = pltpu.SemaphoreType.DMA
    half = width // 2
    prefill, decoded = pl.pallas_call(
        kernel,
        out_shape=(
            jax.ShapeDtypeStruct(prompt_q.shape, BF16),
            jax.ShapeDtypeStruct(sample_states.shape, BF16),
        ),
        in_specs=[hbm, hbm, hbm, vmem, vmem, vmem, vmem, smem, hbm, vmem, hbm, vmem, hbm, vmem, hbm],
        out_specs=(vmem, vmem),
        scratch_shapes=[
            pltpu.VMEM((2, 16, 8, 2, 64, HEAD_DIM), BF16),
            pltpu.VMEM((2, 8, 2, 64, HEAD_DIM), BF16),
            pltpu.VMEM((2, 8, 2, 64, HEAD_DIM), BF16),
            pltpu.VMEM((2, TILE, CHUNK), F32),
            pltpu.VMEM((2, CHUNK, HEAD_DIM), F32),
            pltpu.VMEM((2, CHUNK, HEAD_DIM), F32),
            pltpu.VMEM((2, CHUNK, HEAD_DIM), F32),
            pltpu.VMEM(w_query.shape, BF16),
            pltpu.VMEM(w_key.shape[::-1], BF16),
            pltpu.VMEM(w_value.shape[::-1], BF16),
            pltpu.VMEM(w_out.shape, BF16),
            pltpu.VMEM((rows, HEAD_DIM), BF16),
            pltpu.VMEM((4, rows, HEAD_DIM), BF16),
            pltpu.VMEM((2, rows, HEAD_DIM), F32),
            pltpu.VMEM((3, 2, rows, HEAD_DIM), F32),
            pltpu.VMEM((4, 2, rows, HEAD_DIM), F32),
            pltpu.VMEM((4, 2, rows, HEAD_DIM), F32),
            pltpu.VMEM((2, rows, half), F32),
            pltpu.VMEM((rows, half), F32),
            pltpu.VMEM((16, 48, HEAD_DIM), BF16),
            pltpu.VMEM((16, 48, HEAD_DIM), BF16),
            pltpu.VMEM((16, 48, HEAD_DIM), BF16),
            pltpu.VMEM((16, 48, HEAD_DIM), BF16),
            pltpu.VMEM((4, 4 * rows, CHUNK), F32),
            pltpu.VMEM((rows, width), F32),
            pltpu.VMEM(prompt_q.shape, BF16),
            pltpu.VMEM(prompt_k.shape, BF16),
            pltpu.VMEM(prompt_v.shape, BF16),
            dma((3,)),
            dma((4,)),
            dma((2,)), dma((2,)), dma((2,)),
            dma((2,)), dma((2,)),
            dma((4, 4, 2)), dma((5, 4)), dma((4, 4)), dma((4, 4)),
            dma, dma((2,)),
            dma((4,)), dma((4,)),
            dma((3,)), dma((3,)),
            dma((4,)), dma((4,)),
            dma, dma, dma((16,)), dma((16,)), dma, dma((16,)), dma, dma,
        ],
        compiler_params=pltpu.CompilerParams(
            collective_id=0, has_side_effects=True, vmem_limit_bytes=56 * 2**20
        ),
    )(
        prompt_q, prompt_k, prompt_v, sample_states, norm_gain.reshape(-1, 128),
        cosine, sine, lengths, w_query, b_query[None], w_key.T, b_key[None],
        w_value.T, b_value[None], w_out,
    )
    return pl.pallas_call(
        hand_over,
        out_shape=(
            jax.ShapeDtypeStruct(prefill.shape, BF16),
            jax.ShapeDtypeStruct(decoded.shape, BF16),
        ),
        in_specs=[vmem, vmem],
        out_specs=(vmem, vmem),
    )(prefill, decoded)


def solution(mesh):
    in_specs = (
        P(("grp", "tp"), None),
        P(("grp", "tp"), None),
        P(("grp", "tp"), None),
        P("grp"),
        P("grp", None, None),
        P(),
        P(None, "tp"),
        P("tp"),
        P(None, "tp"),
        P("tp"),
        P(None, "tp"),
        P("tp"),
        P("tp", None),
    )
    out_specs = (P(("grp", "tp"), None), P("grp", None, None))
    return jax.shard_map(shards, mesh=mesh, in_specs=in_specs, out_specs=out_specs, check_vma=False)
```

```python
import math

import jax
import jax.numpy as jnp
from jax import lax
from jax.experimental import pallas as pl
from jax.experimental.pallas import tpu as pltpu
from jax.sharding import PartitionSpec as P

HEADS = 32
KV_HEADS = 8
HEAD_DIM = 128
STEPS = 2
EPSILON = 1e-06
ROPE_BASE = 1000000.0
MESH = pl.DeviceIdType.MESH
F32 = jnp.float32
BF16 = jnp.bfloat16
NEG = -1e30
C = math.log2(math.e) / math.sqrt(HEAD_DIM)
NT = (((1,), (1,)), ((), ()))
CHUNK = 1024
TILE = 256


def dot_nt(a, b):
    return lax.dot_general(a, b, NT, preferred_element_type=F32)


def kernel(
    q_ref, k_ref, v_ref, st_ref, gain_ref, cos_ref, sin_ref, len_ref,
    wq_ref, bq_ref, wk_ref, bk_ref, wv_ref, bv_ref, wo_ref,
    out_ref, dec_ref,
    kvbuf, qbuf, obuf, S, acc, mx, ls,
    wq_v, wk_v, wv_v, wo_v, dq_own, dq, kvp_own, kvp, pmsg, part, opart, rs0, slabs, rs, fbuf, fsib,
    SD, stv, q_v, k_v, v_v,
    in_sem, w_sem, kv0_recv, kv0_loc, kv0_send, q_recv, q_send, ag_recv, ag_send, sib_recv, sib_send,
    o_recv, o_send, dq_recv, dq_send, kvp_recv, kvp_send, part_recv, part_send,
    rs0_recv, rs0_send, rs_recv, rs_send, f_recv, f_send, fs_recv, fs_send,
):
    g = lax.axis_index("grp")
    t = lax.axis_index("tp")
    x, ylo = lax.rem(g, 4), lax.div(g, 4)
    yhi, z, core = lax.div(t, 16), lax.rem(lax.div(t, 2), 8), lax.rem(t, 2)
    y = yhi * 2 + ylo
    own = (ylo * 4 + x) * 2 + yhi

    def dev(xx, yy, zz, cc):
        return {"grp": lax.rem(yy, 2) * 4 + xx, "tp": lax.div(yy, 2) * 16 + zz * 2 + cc}

    def flip(bit, by):
        return bit + by * (1 - 2 * bit)

    def column(by):
        return x + by * (3 - 2 * x), y + by * (3 - 2 * y)

    def rcopy(src, dst, send, recv, to):
        return pltpu.make_async_remote_copy(
            src_ref=src, dst_ref=dst, send_sem=send, recv_sem=recv, device_id=to, device_id_type=MESH
        )

    def drain(ref, sem):
        pltpu.make_async_copy(ref, ref, sem).wait()

    def head_cols(ref, h, width=HEAD_DIM):
        return ref.at[:, pl.ds(pl.multiple_of(h * width, width), width)]

    half = wo_v.shape[1] // 2

    loads = [
        pltpu.make_async_copy(a, b, in_sem.at[i])
        for i, (a, b) in enumerate(((k_ref, k_v), (v_ref, v_v), (q_ref, q_v)))
    ]
    for c in loads:
        c.start()
    weights = [
        pltpu.make_async_copy(a, b, w_sem.at[i])
        for i, (a, b) in enumerate(((wq_ref, wq_v), (wk_ref, wk_v), (wv_ref, wv_v), (wo_ref, wo_v)))
    ]
    for w in weights:
        w.start()

    barrier = pltpu.get_barrier_semaphore()

    def greet(to):
        pl.semaphore_signal(barrier, inc=1, device_id=to, device_id_type=MESH)

    y2 = lax.rem(y + 2, 4)
    for dc in range(2):
        for dz in range(8):
            zz, cc = lax.rem(z + dz, 8), flip(core, dc)
            if dz or dc:
                greet(dev(x, y, zz, cc))
            greet(dev(3 - x, 3 - y, zz, cc))
            greet(dev(x, y2, zz, cc))
    for d in (1, 3):
        greet(dev(lax.rem(x + d, 4), y, z, core))
        greet(dev(x, lax.rem(y + d, 4), z, core))
    for c in loads:
        c.wait()
    pl.semaphore_wait(barrier, 51)

    for dz in (4, 3, 5, 2, 6, 1, 7):
        zz = lax.rem(z + dz, 8)
        for kv, ref in enumerate((k_v, v_v)):
            rcopy(
                head_cols(ref, zz), kvbuf.at[kv, own, z, core], kv0_send.at[kv], kv0_recv.at[kv],
                dev(x, y, zz, core),
            ).start()
    kv_local = [
        pltpu.make_async_copy(head_cols(ref, z), kvbuf.at[kv, own, z, core], kv0_loc.at[kv])
        for kv, ref in enumerate((k_v, v_v))
    ]
    for c in kv_local:
        c.start()
    def send_queries(dp):
        px, py = column(dp)
        for dz in (4, 3, 5, 2, 6, 1, 7, 0):
            zz = lax.rem(z + dz, 8)
            for dc in range(2):
                cc = flip(core, dc)
                src = head_cols(q_v, 4 * zz + 2 * flip(ylo, dp) + cc)
                dst = qbuf.at[ylo, z, core]
                if dz or dp or dc:
                    rcopy(src, dst, q_send.at[dp], q_recv.at[ylo], dev(px, py, zz, cc)).start()
                else:
                    pltpu.make_async_copy(src, dst, q_recv.at[ylo]).start()

    send_queries(0)

    for s in range(16):
        stv[pl.ds(2 * s, 2), :] = st_ref[s].astype(F32)
    states = stv[...]
    scale = lax.rsqrt(jnp.mean(states * states, axis=1, keepdims=True) + EPSILON)
    normed = jnp.concatenate(
        [
            (states[:, j * 128 : (j + 1) * 128] * scale * gain_ref[j : j + 1, :].astype(F32)).astype(BF16)
            for j in range(states.shape[1] // 128)
        ],
        axis=1,
    )
    for w in weights:
        w.wait()
    odd = lax.rem(lax.broadcasted_iota(jnp.int32, (32, HEAD_DIM), 0), 2) == 1
    cosine = jnp.concatenate([cos_ref[...], cos_ref[...]], axis=1)
    sine = jnp.concatenate([-sin_ref[...], sin_ref[...]], axis=1)
    cosine = jnp.where(odd, cosine[1:2, :], cosine[0:1, :])
    sine = jnp.where(odd, sine[1:2, :], sine[0:1, :])

    def rotate(value):
        return value * cosine + pltpu.roll(value, HEAD_DIM // 2, 1) * sine

    query = jnp.dot(normed, wq_v[...], preferred_element_type=F32) + bq_ref[...].astype(F32)
    dq_own[...] = rotate(query).astype(BF16)
    quarter = lax.rem(t, 4)
    spread = (
        lax.broadcasted_iota(jnp.int32, (32, HEAD_DIM), 1)
        == lax.broadcasted_iota(jnp.int32, (32, HEAD_DIM), 0) + quarter * 32
    ).astype(F32)
    for i, (w, b) in enumerate(((wk_v, bk_ref), (wv_v, bv_ref))):
        narrow = dot_nt(normed, w[...]) + b[...].astype(F32)
        kvp_own[i] = jnp.dot(narrow, spread, precision=lax.Precision.HIGHEST, preferred_element_type=F32)

    def to_tp(target, src, dst, send, recv):
        @pl.when(target != t)
        def _():
            rcopy(src, dst, send, recv, {"grp": g, "tp": target}).start()

        @pl.when(target == t)
        def _():
            pltpu.make_async_copy(src, dst, recv).start()

    for i in range(4):
        target = (i // 2) * 16 + lax.div(t, 4) * 2 + i % 2
        to_tp(target, dq_own, dq.at[quarter], dq_send.at[i], dq_recv.at[quarter])
    for m in range(1, 4):
        target = lax.div(t, 4) * 4 + lax.rem(quarter + m, 4)
        rcopy(kvp_own, kvp.at[m - 1], kvp_send.at[m - 1], kvp_recv.at[m - 1], {"grp": g, "tp": target}).start()

    acc[...] = jnp.zeros_like(acc)
    mx[...] = jnp.full_like(mx, NEG)
    ls[...] = jnp.zeros_like(ls)

    def place(o1, o2):
        ox, oy = (1 - core) * o1 + core * o2, core * o1 + (1 - core) * o2
        return lax.rem(x + ox, 4), lax.rem(y + oy, 4)

    def chunk_of(o1, o2):
        xx, yy = place(o1, o2)
        return (lax.rem(yy, 2) * 4 + xx) * 2 + lax.div(yy, 2)

    def block(o1, o2, kv=None):
        return kvbuf.at[slice(None) if kv is None else kv, chunk_of(o1, o2), :, core]

    def toward(axis, step):
        xx, yy = place(step, 0) if axis == 1 else place(0, step)
        return dev(xx, yy, z, core)

    def send(src, sem, recv, to):
        rcopy(src, src, sem, recv, to).start()

    sibling = dev(x, y, z, 1 - core)

    def to_sibling(o1, o2):
        send(block(o1, o2), sib_send.at[o1, o2], sib_recv.at[o1, o2], sibling)

    def from_sibling(o1, o2):
        drain(kvbuf.at[:, chunk_of(o1, o2), :, 1 - core], sib_recv.at[o2, o1])

    def open_axis1():
        send(block(0, 0), ag_send.at[0, 0], ag_recv.at[3, 0, 0], toward(1, 1))
        send(block(0, 0), ag_send.at[0, 1], ag_recv.at[1, 0, 0], toward(1, 3))

    def open_axis2(o1):
        send(block(o1, 0), ag_send.at[1 + o1, 0], ag_recv.at[o1, 3, 0], toward(2, 1))
        send(block(o1, 0), ag_send.at[1 + o1, 1], ag_recv.at[o1, 1, 0], toward(2, 3))

    def pass_axis1():
        drain(block(3, 0), ag_recv.at[3, 0, 0])
        send(block(3, 0, 0), ag_send.at[0, 2], ag_recv.at[2, 0, 0], toward(1, 1))
        drain(block(1, 0), ag_recv.at[1, 0, 0])
        send(block(1, 0, 1), ag_send.at[0, 3], ag_recv.at[2, 0, 1], toward(1, 3))

    def pass_axis2(o1):
        drain(block(o1, 3), ag_recv.at[o1, 3, 0])
        send(block(o1, 3, 0), ag_send.at[1 + o1, 2], ag_recv.at[o1, 2, 0], toward(2, 1))
        drain(block(o1, 1), ag_recv.at[o1, 1, 0])
        send(block(o1, 1, 1), ag_send.at[1 + o1, 3], ag_recv.at[o1, 2, 1], toward(2, 3))
        to_sibling(o1, 3)
        to_sibling(o1, 1)

    def end_axis(o1, o2):
        for kv in range(2):
            drain(block(o1, o2, kv), ag_recv.at[o1, o2, kv])
        to_sibling(o1, o2)

    for kv in range(2):
        kv_local[kv].wait()
        drain(kvbuf.at[kv, own, pl.ds(0, 7), core], kv0_recv.at[kv])
    open_axis1()
    open_axis2(0)
    to_sibling(0, 0)
    send_queries(1)

    low = own + ylo * (15 - 2 * own)

    def unit(slot, cc, diagonal):
        tiles = CHUNK // TILE
        keys = kvbuf[0, cc].reshape(CHUNK, HEAD_DIM)
        values = kvbuf[1, cc].reshape(CHUNK, HEAD_DIM)
        held = {}

        def scores(i):
            width = (i + 1) * TILE if diagonal else CHUNK
            rows = pl.ds(i * TILE, TILE)
            s = dot_nt(qbuf[slot, 2 * i : 2 * i + 2].reshape(TILE, HEAD_DIM), keys[:width])
            if diagonal:
                r = lax.broadcasted_iota(jnp.int32, (TILE, width), 0) + i * TILE
                s = jnp.where(lax.broadcasted_iota(jnp.int32, (TILE, width), 1) <= r, s, NEG)
            S[i % 2, :, :width] = s
            old = mx[slot, rows, :]
            new = jnp.maximum(old, jnp.max(s, axis=1, keepdims=True))
            mx[slot, rows, :] = new
            held[i] = (old, new)

        def mix(i):
            width = (i + 1) * TILE if diagonal else CHUNK
            rows = pl.ds(i * TILE, TILE)
            old, new = held.pop(i)
            p = jnp.exp2(S[i % 2, :, :width] * C - (new * C)[:, :1])
            shrink = jnp.exp2((old - new) * C)
            ls[slot, rows, :] = ls[slot, rows, :] * shrink + jnp.sum(p, axis=1, keepdims=True)
            gained = jnp.dot(p.astype(BF16), values[:width], preferred_element_type=F32)
            acc[slot, rows, :] = acc[slot, rows, :] * shrink + gained

        scores(0)
        for i in range(tiles):
            if i + 1 < tiles:
                scores(i + 1)
            mix(i)

    def send_output(slot):
        obuf[slot] = (acc[slot] / ls[slot]).astype(BF16).reshape(8, 2, 64, HEAD_DIM)
        dp = flip(slot, ylo)
        px, py = column(dp)
        for dz in range(8):
            zz = lax.rem(z + dz, 8)
            for dc in range(2):
                cc = flip(core, dc)
                src = obuf.at[slot, zz, cc]
                dst = head_cols(out_ref, 4 * z + 2 * ylo + core)

                def away(src=src, dst=dst, to=dev(px, py, zz, cc), dp=dp):
                    rcopy(src, dst, o_send.at[dp], o_recv, to).start()

                if dz or dc:
                    away()
                else:
                    pl.when(dp == 1)(away)

                    @pl.when(dp == 0)
                    def _():
                        pltpu.make_async_copy(src, dst, o_recv).start()

    def decode_attend():
        for i in range(4):
            drain(dq.at[i], dq_recv.at[i])
        limit = len_ref[0]
        yq = lax.rem(y + core, 4)
        queries = dq[...].reshape(128, HEAD_DIM)
        chunks = [(lax.rem(yq, 2) * 4 + i) * 2 + lax.div(yq, 2) for i in range(4)]
        top = jnp.full((128, 1), NEG, F32)
        for i, cc in enumerate(chunks):
            s = dot_nt(queries, kvbuf[0, cc].reshape(CHUNK, HEAD_DIM))
            allowed = lax.broadcasted_iota(jnp.int32, (128, CHUNK), 1) + cc * CHUNK < limit
            s = jnp.where(allowed, s, NEG)
            SD[i] = s
            top = jnp.maximum(top, jnp.max(s, axis=1, keepdims=True))
        total = jnp.zeros((128, 1), F32)
        mixed = jnp.zeros((128, HEAD_DIM), F32)
        for i, cc in enumerate(chunks):
            s = SD[i]
            p = jnp.where(s > 0.5 * NEG, jnp.exp2(s * C - top * C), 0.0)
            total = total + jnp.sum(p, axis=1, keepdims=True)
            mixed = mixed + jnp.dot(
                p.astype(BF16), kvbuf[1, cc].reshape(CHUNK, HEAD_DIM), preferred_element_type=F32
            )
        first = lax.broadcasted_iota(jnp.int32, (32, HEAD_DIM), 1) < 64
        for i in range(4):
            rows = slice(i * 32, i * 32 + 32)
            pmsg[i, 0] = mixed[rows]
            pmsg[i, 1] = jnp.where(first, top[rows], total[rows])
        for i in range(4):
            slot = yhi * 2 + core
            to_tp(4 * z + i, pmsg.at[i], part.at[slot], part_send.at[i], part_recv.at[slot])

    def decode_join():
        for i in range(4):
            drain(part.at[i], part_recv.at[i])
        for i in range(3):
            drain(kvp.at[i], kvp_recv.at[i])
        step_key = rotate(kvp_own[0] + kvp[0, 0] + kvp[1, 0] + kvp[2, 0]).astype(BF16).astype(F32)
        step_value = (kvp_own[1] + kvp[0, 1] + kvp[1, 1] + kvp[2, 1]).astype(BF16).astype(F32)
        step_query = dq_own[...].astype(F32)
        here = jnp.sum(step_query * step_key, axis=1, keepdims=True)
        before = jnp.sum(step_query * pltpu.roll(step_key, 1, 0), axis=1, keepdims=True)
        later = lax.rem(lax.broadcasted_iota(jnp.int32, (32, 1), 0), 2) == 1
        before = jnp.where(later, before, NEG)
        tops = [part[i, 1][:, :1] for i in range(4)]
        sums = [part[i, 1][:, 64:65] for i in range(4)]
        top = jnp.maximum(here, before)
        for m in tops:
            top = jnp.maximum(top, m)
        p_here = jnp.exp2((here - top) * C)
        p_before = jnp.where(later, jnp.exp2((before - top) * C), 0.0)
        total = p_here + p_before
        mixed = p_here.astype(BF16).astype(F32) * step_value
        mixed = mixed + p_before.astype(BF16).astype(F32) * pltpu.roll(step_value, 1, 0)
        for i in range(4):
            w = jnp.exp2((tops[i] - top) * C)
            total = total + w * sums[i]
            mixed = mixed + w * part[i, 0]
        attended = (mixed / total).astype(BF16)
        for i in range(2):
            opart[i] = jnp.dot(attended, wo_v[:, i * half : (i + 1) * half], preferred_element_type=F32)
        rcopy(opart.at[1 - core], rs0, rs0_send, rs0_recv, sibling).start()

    mine = yhi * 8 + z

    def decode_sum():
        drain(rs0, rs0_recv)
        both = opart[core] + rs0[...]
        for n in range(16):
            rows, first = slice(n // 4 * 8, n // 4 * 8 + 8), n % 4 * 640
            pieces = [both[rows, first + j * 128 : first + j * 128 + 128] for j in range(5)]
            slabs[n] = jnp.concatenate(pieces + pieces[:1], axis=0).astype(BF16)
        for n in range(16):
            zz, yy = lax.rem(z + n % 8, 8), flip(yhi, n // 8)
            src = slabs.at[yy * 8 + zz]
            if n:
                rcopy(src, rs.at[n], rs_send.at[n], rs_recv.at[n], dev(x, yy * 2 + ylo, zz, core)).start()
            else:
                pltpu.make_async_copy(src, rs.at[0], rs_recv.at[0]).start()

    def decode_spread():
        for n in range(16):
            drain(rs.at[n], rs_recv.at[n])
        total_rows = rs[0].astype(F32)
        for n in range(1, 16):
            total_rows = total_rows + rs[n].astype(F32)
        slabs[mine] = total_rows.astype(BF16)
        for n in range(16):
            zz, yy = lax.rem(z + n % 8, 8), flip(yhi, n // 8)
            if n:
                rcopy(slabs.at[mine], fbuf.at[mine], f_send.at[n], f_recv, dev(x, yy * 2 + ylo, zz, core)).start()
            else:
                pltpu.make_async_copy(slabs.at[mine], fbuf.at[mine], f_recv).start()

    def decode_swap():
        drain(fbuf, f_recv)
        rcopy(fbuf, fsib, fs_send, fs_recv, sibling).start()

    def decode_finish():
        drain(fsib, fs_recv)
        here = lax.broadcasted_iota(jnp.int32, fbuf.shape[1:], 0) * 0 + core == 0
        for part_no in range(2):
            for group in range(4):
                pieces = []
                for n in range(4 * group, 4 * group + 4):
                    a, b = (fbuf, fsib) if part_no == 0 else (fsib, fbuf)
                    block_rows = jnp.where(here, a[n].astype(F32), b[n].astype(F32))
                    pieces += [block_rows[8 * j : 8 * j + 8] for j in range(5)]
                rows = jnp.concatenate(pieces, axis=1).astype(BF16)
                for r in range(4):
                    dec_ref[4 * group + r, :, part_no * half : (part_no + 1) * half] = rows[2 * r : 2 * r + 2]

    order = (
        (0, 0), (1, 0), (0, 1), (3, 0), (0, 3), (2, 0), (0, 2), (1, 1), (1, 3),
        (3, 1), (3, 3), (1, 2), (2, 1), (3, 2), (2, 3), (2, 2),
    )
    early = 9

    def look_up(table, v):
        found = v * 0 + table[0]
        for n in range(1, len(table)):
            found = jnp.where(v == n, table[n], found)
        return found

    def place_of(v):
        return look_up([o[0] for o in order], v), look_up([o[1] for o in order], v)

    def hop1():
        pass_axis1()
        open_axis2(1)
        open_axis2(3)
        to_sibling(1, 0)
        to_sibling(3, 0)
        pass_axis2(0)

    def hop2():
        end_axis(2, 0)
        open_axis2(2)

    def hop3():
        pass_axis2(1)
        pass_axis2(3)

    def hop4():
        end_axis(0, 2)

    def hop5():
        pass_axis2(2)

    def hop6():
        end_axis(1, 2)
        end_axis(3, 2)
        end_axis(2, 2)

    def item(i):
        second = i >= 16 + early
        slot = jnp.where(i < 2 * early, lax.rem(i, 2), jnp.where(second, 1, 0))
        v = jnp.where(i < 2 * early, lax.div(i, 2), jnp.where(second, i - 16, i - early))
        o1, o2 = place_of(v)
        return slot, v, o1, o2, chunk_of(o1, o2), low + slot * (15 - 2 * low)

    hops = ((2, hop2), (3, hop3), (3, hop4), (4, hop5), (5, hop6))
    steps = (
        (6, decode_attend), (8, decode_join), (9, decode_sum), (13, decode_spread),
    )

    def work(u, carry):
        at, level, seen = carry

        def skips(i):
            slot, v, o1, o2, cc, last = item(i)
            return cc > last

        now = lax.while_loop(skips, lambda i: i + 1, at)
        slot, v, o1, o2, cc, last = item(now)
        due = look_up((1, 2, 2, 3, 3, 4, 5), jnp.minimum(u, 6))
        due = jnp.maximum(due, jnp.where(v <= 4, 1, jnp.where(v <= 10, 3, 5)))
        for needs, hop in hops:
            pl.when((level < needs) & (needs <= due))(hop)
        known = jnp.where(u == 6, 16, jnp.maximum(seen, v + 1))

        def learn(n, c):
            from_sibling(*place_of(n))
            return c

        lax.fori_loop(seen, known, learn, 0)
        pl.when((at <= 16 + early) & (now >= 16 + early))(lambda: send_output(0))
        for when, step in steps:
            pl.when(u == when)(step)

        @pl.when(cc < last)
        def _():
            unit(slot, cc, False)

        @pl.when(cc == last)
        def _():
            unit(slot, cc, True)

        return now + 1, jnp.maximum(level, due), known

    drain(qbuf.at[ylo], q_recv.at[ylo])

    def all_work(u, carry):
        @pl.when(u == 1)
        def _():
            hop1()
            drain(qbuf.at[1 - ylo], q_recv.at[1 - ylo])

        return work(u, carry)

    zero = t * 0
    lax.fori_loop(0, 17, all_work, (zero, zero + 1, zero))
    send_output(1)
    decode_swap()
    decode_finish()

    for n in range(1, 16):
        drain(rs.at[n], rs_send.at[n])
        drain(rs.at[n], f_send.at[n])
    for i in range(4):
        pl.when((i // 2) * 16 + lax.div(t, 4) * 2 + i % 2 != t)(lambda i=i: drain(dq_own, dq_send.at[i]))
        pl.when(4 * z + i != t)(lambda i=i: drain(pmsg.at[i], part_send.at[i]))
    for i in range(3):
        drain(kvp_own, kvp_send.at[i])
    for kv in range(2):
        drain(kvbuf.at[0, pl.ds(0, 7), 0, 0], kv0_send.at[kv])
    drain(kvbuf.at[0, pl.ds(0, 15), 0, 0], q_send.at[0])
    drain(kvbuf.at[0, pl.ds(0, 16), 0, 0], q_send.at[1])
    drain(kvbuf.at[0, pl.ds(0, 15), 0, 0], o_send.at[0])
    drain(kvbuf.at[0, pl.ds(0, 16), 0, 0], o_send.at[1])
    whole, half_block = kvbuf.at[:, 0, :, 0], kvbuf.at[0, 0, :, 0]
    for a in range(5):
        for b in range(4):
            drain(whole if b < 2 else half_block, ag_send.at[a, b])
    for o1 in range(4):
        for o2 in range(4):
            drain(whole, sib_send.at[o1, o2])
    drain(rs0, rs0_send)
    drain(fbuf, fs_send)
    drain(out_ref, o_recv)


def hand_over(a_ref, b_ref, out_ref, dec_ref):
    out_ref[...] = a_ref[...]
    dec_ref[...] = b_ref[...]


def shards(
    prompt_q, prompt_k, prompt_v, lengths, sample_states, norm_gain,
    w_query, b_query, w_key, b_key, w_value, b_value, w_out,
):
    samples, steps, width = sample_states.shape
    rows = samples * steps
    half_dim = HEAD_DIM // 2
    positions = (lengths[0] + jnp.arange(steps, dtype=jnp.int32)).astype(F32)[:, None]
    frequency = ROPE_BASE ** (-(2.0 * jnp.arange(half_dim, dtype=F32)) / HEAD_DIM)
    angles = positions * frequency
    cosine, sine = jnp.cos(angles), jnp.sin(angles)
    vmem = pl.BlockSpec(memory_space=pltpu.VMEM)
    smem = pl.BlockSpec(memory_space=pltpu.SMEM)
    hbm = pl.BlockSpec(memory_space=pl.ANY)
    dma = pltpu.SemaphoreType.DMA
    half = width // 2
    prefill, decoded = pl.pallas_call(
        kernel,
        out_shape=(
            jax.ShapeDtypeStruct(prompt_q.shape, BF16),
            jax.ShapeDtypeStruct(sample_states.shape, BF16),
        ),
        in_specs=[hbm, hbm, hbm, vmem, vmem, vmem, vmem, smem, hbm, vmem, hbm, vmem, hbm, vmem, hbm],
        out_specs=(vmem, vmem),
        scratch_shapes=[
            pltpu.VMEM((2, 16, 8, 2, 64, HEAD_DIM), BF16),
            pltpu.VMEM((2, 8, 2, 64, HEAD_DIM), BF16),
            pltpu.VMEM((2, 8, 2, 64, HEAD_DIM), BF16),
            pltpu.VMEM((2, TILE, CHUNK), F32),
            pltpu.VMEM((2, CHUNK, HEAD_DIM), F32),
            pltpu.VMEM((2, CHUNK, HEAD_DIM), F32),
            pltpu.VMEM((2, CHUNK, HEAD_DIM), F32),
            pltpu.VMEM(w_query.shape, BF16),
            pltpu.VMEM(w_key.shape[::-1], BF16),
            pltpu.VMEM(w_value.shape[::-1], BF16),
            pltpu.VMEM(w_out.shape, BF16),
            pltpu.VMEM((rows, HEAD_DIM), BF16),
            pltpu.VMEM((4, rows, HEAD_DIM), BF16),
            pltpu.VMEM((2, rows, HEAD_DIM), F32),
            pltpu.VMEM((3, 2, rows, HEAD_DIM), F32),
            pltpu.VMEM((4, 2, rows, HEAD_DIM), F32),
            pltpu.VMEM((4, 2, rows, HEAD_DIM), F32),
            pltpu.VMEM((2, rows, half), F32),
            pltpu.VMEM((rows, half), F32),
            pltpu.VMEM((16, 48, HEAD_DIM), BF16),
            pltpu.VMEM((16, 48, HEAD_DIM), BF16),
            pltpu.VMEM((16, 48, HEAD_DIM), BF16),
            pltpu.VMEM((16, 48, HEAD_DIM), BF16),
            pltpu.VMEM((4, 4 * rows, CHUNK), F32),
            pltpu.VMEM((rows, width), F32),
            pltpu.VMEM(prompt_q.shape, BF16),
            pltpu.VMEM(prompt_k.shape, BF16),
            pltpu.VMEM(prompt_v.shape, BF16),
            dma((3,)),
            dma((4,)),
            dma((2,)), dma((2,)), dma((2,)),
            dma((2,)), dma((2,)),
            dma((4, 4, 2)), dma((5, 4)), dma((4, 4)), dma((4, 4)),
            dma, dma((2,)),
            dma((4,)), dma((4,)),
            dma((3,)), dma((3,)),
            dma((4,)), dma((4,)),
            dma, dma, dma((16,)), dma((16,)), dma, dma((16,)), dma, dma,
        ],
        compiler_params=pltpu.CompilerParams(
            collective_id=0, has_side_effects=True, vmem_limit_bytes=56 * 2**20
        ),
    )(
        prompt_q, prompt_k, prompt_v, sample_states, norm_gain.reshape(-1, 128),
        cosine, sine, lengths, w_query, b_query[None], w_key.T, b_key[None],
        w_value.T, b_value[None], w_out,
    )
    return pl.pallas_call(
        hand_over,
        out_shape=(
            jax.ShapeDtypeStruct(prefill.shape, BF16),
            jax.ShapeDtypeStruct(decoded.shape, BF16),
        ),
        in_specs=[vmem, vmem],
        out_specs=(vmem, vmem),
    )(prefill, decoded)


def solution(mesh):
    in_specs = (
        P(("grp", "tp"), None),
        P(("grp", "tp"), None),
        P(("grp", "tp"), None),
        P("grp"),
        P("grp", None, None),
        P(),
        P(None, "tp"),
        P("tp"),
        P(None, "tp"),
        P("tp"),
        P(None, "tp"),
        P("tp"),
        P("tp", None),
    )
    out_specs = (P(("grp", "tp"), None), P("grp", None, None))
    return jax.shard_map(shards, mesh=mesh, in_specs=in_specs, out_specs=out_specs, check_vma=False)
```
